32 devices in a mesh: pass: 8 (over y, x, core), kv: 4 (over z).
Axes of the slice: x: 2, y: 2, z: 4, core: 2. Of those that a mesh axis runs over, the one named last changes fastest.
Arguments:
- queries: bfloat16 [8, 64, 4096], P('pass', None, 'kv'), may hold values from -40 to 40
- suffix_keys: bfloat16 [8, 64, 512], P('pass', None, 'kv'), may hold values from -5 to 5
- suffix_values: bfloat16 [8, 64, 512], P('pass', None, 'kv'), may hold values from -40 to 40
- passage_keys: bfloat16 [32, 1024, 512], P('pass', None, 'kv'), may hold values from -5 to 5
- passage_values: bfloat16 [32, 1024, 512], P('pass', None, 'kv'), may hold values from -40 to 40
- fresh_keys: bfloat16 [8, 8, 128, 512], P('pass', None, None, 'kv'), may hold values from -5 to 5
- fresh_values: bfloat16 [8, 8, 128, 512], P('pass', None, None, 'kv'), may hold values from -40 to 40
- citations: int32 [8, 8], P('pass'), may hold values from 0 to 31, all different within a row; in each aligned block of 8 rows (0 to 7, 8 to 15, ...) at most 4 rows name the same one
- selected: int32 [8, 8, 128], P('pass'), may hold values from 0 to 1023, as said below
Outputs:
- attention: bfloat16 [8, 64, 4096], P('pass', 'kv')
The draws below stay inside these ranges and needn't reach their ends.
Inputs may be any that keep to these rules, and one draw needn't show every extreme that they name: `citations`: each request cites 8 distinct passages; every passage is cited; no passage is cited by more than 4 requests, a bound that some block reaches. `selected`: each list holds 128 distinct positions of its passage.
All inputs are finite; a program needn't handle non-finite values.
Results may differ from the reference program's by a relative error of at most 0.0053.
Values may be sent and summed in bfloat16 or wider, within the bound.
A program may use at most 128 MiB of HBM per device.

```python
import math
import jax
import jax.numpy as jnp
import numpy as np
from jax import lax

HD = 128
GROUP = 8
L = 1024
CITE = 8
SEL = 128
S = 64
PASS_DEV = 4
PMOST = 4
KVH = 4
REQ = 8
PASSAGES = 32


def suffix_pair(key):
    key_rows = jnp.clip(jax.random.normal(jax.random.fold_in(key, 11), (REQ, S, KVH, HD), jnp.float32), -5.0, 5.0)
    query_rows = 1.5 * jnp.clip(jax.random.normal(jax.random.fold_in(key, 12), (REQ, S, KVH, GROUP, HD), jnp.float32), -5.0, 5.0)
    return (query_rows.reshape(REQ, S, KVH * GROUP * HD), key_rows.reshape(REQ, S, KVH * HD))


def draw_queries(key, part):
    return suffix_pair(key)[0].astype(jnp.bfloat16)


def draw_suffix_keys(key, part):
    return suffix_pair(key)[1].astype(jnp.bfloat16)


def draw_passage_keys(key, part):
    rows = jnp.clip(jax.random.normal(jax.random.fold_in(key, 41), (PASSAGES, L, KVH, HD), jnp.float32), -5.0, 5.0)
    return rows.reshape(PASSAGES, L, KVH * HD).astype(jnp.bfloat16)


def draw_selected(key, part):
    base_key = jax.random.fold_in(key, 21)
    row_keys = jax.random.split(base_key, REQ * CITE)
    picked = jax.vmap(lambda row_key: jax.random.permutation(row_key, L)[:SEL])(row_keys)
    return picked.reshape(REQ, CITE, SEL).astype(jnp.int32)


def block_scale(stream_key, shape, cuts, low, top_value):
    def one(position, blocks):
        steps = jax.random.uniform(jax.random.fold_in(jax.random.fold_in(stream_key, 6), position), (blocks,), jnp.float32, low / len(cuts), top_value / len(cuts))
        return jnp.repeat(jnp.exp(steps), shape[position] // blocks).reshape((-1,) + (1,) * (len(shape) - position - 1))

    level = one(*cuts[0])
    for cut in cuts[1:]:
        level = level * one(*cut)
    return level


def shared_out(stream_key, own, number, rows, number_of, top, reach, lean):
    ranking = jax.random.permutation(stream_key, number_of)
    crowded, usual = load_shares(number_of, rows * top, reach, lean, True), load_shares(number_of, rows * top, reach, lean, False)
    places = jnp.arange(number_of)

    def named(lengths, rotation):
        used = int((lengths > 0).sum())
        fixed = max(1, used // 4)
        moved = fixed + (places - fixed + rotation * (used - fixed)) % max(1, number_of - fixed)
        return jnp.zeros((number_of,), jnp.int32).at[ranking[jnp.where(places < fixed, places, moved)]].set(jnp.asarray(lengths, jnp.int32))

    lengths = jnp.where(number % 4 == 0, named(crowded, number // 4), named(usual, number - number // 4 - 1))
    mixed = jax.random.permutation(jax.random.fold_in(own, 3), number_of)
    donor, sink = mixed[0:number_of // 2 * 2:2], mixed[1:number_of // 2 * 2:2]
    room = jnp.minimum(lengths[donor] - 1, reach - lengths[sink]) // 2
    room = jnp.where((donor == ranking[0]) | (sink == ranking[0]) | (lengths[sink] == 0), 0, jnp.maximum(room, 0))
    moved = jax.random.randint(jax.random.fold_in(own, 4), (number_of // 2,), 0, 1 << 20) % (room + 1)
    lengths = lengths.at[donor].add(-moved).at[sink].add(moved)
    labels = jnp.searchsorted(jnp.cumsum(lengths), jnp.arange(rows * top), side="right").astype(jnp.int32)
    grid = labels.reshape(top, rows).T
    grid = grid[jax.random.permutation(jax.random.fold_in(own, 1), rows)]
    rotation = jax.random.randint(jax.random.fold_in(own, 2), (rows, 1), 0, top)
    return jnp.take_along_axis(grid, (jnp.arange(top)[None, :] + rotation) % top, axis=1)


def load_shares(count, total, limit, slope, full):
    portions = [(1 << 20) // math.isqrt(standing ** slope) + 1 for standing in range(1, count + 1)]
    largest = limit if full else min(limit, max(-(-total // count), total * portions[0] // sum(portions)))
    least = 1 if total - largest >= count - 1 else 0
    given, spare = [largest] + [least] * (count - 1), total - largest - least * (count - 1)
    while spare > 0:
        candidates = [i for i in range(1, count) if given[i] < largest] or [i for i in range(1, count) if given[i] < limit]
        pool, remaining = sum([portions[i] for i in candidates]), spare
        for i in candidates:
            more = min(limit - given[i], max(1, remaining * portions[i] // pool), spare)
            given[i] = given[i] + more
            spare = spare - more
    return np.array(given)


def bell_draw(rng, extent, width, reach, shards=(), held_as=jnp.bfloat16):
    values = jax.random.normal(rng, extent, jnp.float32) * width
    if len(shards) > 0:
        values = block_scale(rng, extent, shards, -0.22, 0.18) * values
    return jnp.clip(values, min=-reach, max=reach).astype(held_as)


def setup_inputs(seed: int = 0) -> dict:
    key_list = jax.random.split(jax.random.key(seed), 10)
    queries = draw_queries(jax.random.fold_in(key_list[9], 71), 0)
    suffix_keys = draw_suffix_keys(jax.random.fold_in(key_list[9], 71), 0)
    suffix_values = bell_draw(key_list[2], (REQ, S, KVH * HD), 8.0, 40.0, ((0, 8), (2, 4)))
    passage_keys = draw_passage_keys(jax.random.fold_in(key_list[9], 71), 0)
    passage_values = bell_draw(key_list[4], (PASSAGES, L, KVH * HD), 8.0, 40.0, ((0, 8), (2, 4)))
    fresh_keys = bell_draw(key_list[5], (REQ, CITE, SEL, KVH * HD), 1.0, 5.0, ((0, 8), (3, 4)))
    fresh_values = bell_draw(key_list[6], (REQ, CITE, SEL, KVH * HD), 8.0, 40.0, ((0, 8), (3, 4)))
    citations_keys = jax.random.split(jax.random.fold_in(key_list[7], 1), REQ // REQ)
    citations_turns = jax.random.permutation(jax.random.fold_in(key_list[7], 3), REQ // REQ)
    citations = jax.vmap(lambda own, number: shared_out(jax.random.fold_in(key_list[7], 2), own, number, REQ, PASSAGES, CITE, PMOST, 2))(citations_keys, citations_turns).reshape((REQ, CITE))
    selected = draw_selected(jax.random.fold_in(key_list[9], 71), 0)
    return dict(queries=queries, suffix_keys=suffix_keys, suffix_values=suffix_values, passage_keys=passage_keys, passage_values=passage_values, fresh_keys=fresh_keys, fresh_values=fresh_values, citations=citations, selected=selected)


very_low = -1e+30

def rounded_float(array):
    return lax.optimization_barrier(array.astype(jnp.bfloat16)).astype(jnp.float32)

def reference(queries, suffix_keys, suffix_values, passage_keys, passage_values, fresh_keys, fresh_values, citations, selected):
    score_scale = 1.0 / math.sqrt(HD)
    cite_ids = jnp.arange(CITE, dtype=jnp.int32)
    positions = jnp.arange(L, dtype=jnp.int32)
    host_span = S + CITE * SEL
    later = jnp.arange(host_span, dtype=jnp.int32)[None, :]
    causal = (later >= S) | (later <= jnp.arange(S, dtype=jnp.int32)[:, None])
    highest = lax.Precision.HIGHEST

    def one_request(packed):
        query_rows, own_keys, own_values, new_keys, new_values, cite_row, pick_rows = packed
        query_float = query_rows.astype(jnp.float32).reshape(S, KVH, GROUP, HD)
        cached_keys = passage_keys[cite_row].astype(jnp.float32).reshape(CITE, L, KVH, HD)
        cached_values = passage_values[cite_row].astype(jnp.float32).reshape(CITE, L, KVH, HD)
        dropped = jnp.any(pick_rows[:, :, None] == positions[None, None, :], axis=1)
        scores = jnp.einsum('skgd,clkd->ckgsl', query_float, cached_keys, precision=highest) * score_scale
        scores = jnp.where(dropped[:, None, None, None, :], very_low, scores)
        cite_max = lax.optimization_barrier(jnp.max(scores, axis=-1))
        owner_ids = cite_row // PASS_DEV
        same_group = owner_ids[:, None] == owner_ids[None, :]
        group_max = lax.optimization_barrier(jnp.max(jnp.where(same_group[:, :, None, None, None], cite_max[None], very_low), axis=1))
        weights = jnp.exp(scores - group_max[..., None])
        same_float = same_group.astype(jnp.float32)
        group_sum = jnp.einsum('ab,bkgs->akgs', same_float, lax.optimization_barrier(jnp.sum(weights, axis=-1)), precision=highest)
        cite_acc = jnp.einsum('ckgsl,clkd->ckgsd', rounded_float(weights), cached_values, precision=highest)
        group_acc = jnp.einsum('ab,bkgsd->akgsd', same_float, cite_acc, precision=highest)
        group_out = rounded_float(group_acc / group_sum[..., None])
        earlier = same_group & (cite_ids[None, :] < cite_ids[:, None])
        leading = jnp.logical_not(jnp.any(earlier, axis=1))
        host_keys = jnp.concatenate([own_keys, new_keys.reshape(CITE * SEL, KVH * HD)], axis=0).astype(jnp.float32).reshape(host_span, KVH, HD)
        host_values = jnp.concatenate([own_values, new_values.reshape(CITE * SEL, KVH * HD)], axis=0).astype(jnp.float32).reshape(host_span, KVH, HD)
        host_scores = jnp.einsum('skgd,tkd->kgst', query_float, host_keys, precision=highest) * score_scale
        host_scores = jnp.where(causal[None, None], host_scores, very_low)
        host_max = lax.optimization_barrier(jnp.max(host_scores, axis=-1))
        host_weights = jnp.exp(host_scores - host_max[..., None])
        host_sum = lax.optimization_barrier(jnp.sum(host_weights, axis=-1))
        host_acc = jnp.einsum('kgst,tkd->kgsd', rounded_float(host_weights), host_values, precision=highest)
        ceiling = jnp.maximum(host_max, lax.optimization_barrier(jnp.max(group_max, axis=0)))
        shares = jnp.where(leading[:, None, None, None], group_sum * jnp.exp(group_max - ceiling[None]), 0.0)
        near_scale = jnp.exp(host_max - ceiling)
        numerator = host_acc * near_scale[..., None] + lax.optimization_barrier(jnp.sum(shares[..., None] * group_out, axis=0))
        denominator = host_sum * near_scale + lax.optimization_barrier(jnp.sum(shares, axis=0))
        result = numerator / denominator[..., None]
        return result.transpose(2, 0, 1, 3).reshape(S, KVH * GROUP * HD).astype(jnp.bfloat16)
    return lax.map(one_request, (queries, suffix_keys, suffix_values, fresh_keys, fresh_values, citations, selected))
```

```python
import functools
import math

import jax
import jax.numpy as jnp
from jax import lax
from jax.experimental import pallas as pl
from jax.experimental.pallas import tpu as pltpu
from jax.sharding import PartitionSpec as P

HD = 128
MESH = pl.DeviceIdType.MESH
very_low = -1e30
FACTOR = math.log2(math.e) / math.sqrt(HD)
ONES = 16
CHUNK = 256


def nt_dot(a, b):
    return lax.dot_general(a, b, (((1,), (1,)), ((), ())), preferred_element_type=jnp.float32)


def nn_dot(a, b):
    return jnp.dot(a, b, preferred_element_type=jnp.float32)


def stack_heads(rows, group_size):
    return jnp.concatenate([rows[:, g * HD : (g + 1) * HD] for g in range(group_size)], axis=0)


def gather_kernel(
    n,
    q_ref,
    sk_ref,
    sv_ref,
    fk_ref,
    fv_ref,
    cite_ref,
    sel_ref,
    q_all,
    cite_all,
    sel_all,
    host_acc,
    host_max,
    cite_buf,
    own_sem,
    send_sem,
    recv_sem,
    fsend_sem,
    frecv_sem,
):
    me = lax.axis_index("pass")
    chip, core = me // 2, me % 2
    chips = n // 2
    sibling = chip * 2 + (1 - core)

    def peer(off):
        return ((chip + off) % chips) * 2 + core

    def origin(off, lane):
        return ((chip + chips - off) % chips) * 2 + lane

    barrier = pltpu.get_barrier_semaphore()
    for target in [sibling] + [peer(off) for off in range(1, chips)]:
        pl.semaphore_signal(barrier, inc=1, device_id={"pass": target}, device_id_type=MESH)
    cite_buf[...] = jnp.zeros_like(cite_buf)
    cite_buf[0:1, 0 : cite_ref.shape[1]] = cite_ref[...]
    pl.semaphore_wait(barrier, chips)

    sources = (q_ref.at[0], cite_buf, sel_ref.at[0])
    places = (q_all, cite_all, sel_all)

    def remote(i, off, source, slot, target, send, recv):
        return pltpu.make_async_remote_copy(
            src_ref=source,
            dst_ref=places[i].at[slot],
            send_sem=send.at[i, off],
            recv_sem=recv.at[i, off],
            device_id={"pass": target},
            device_id_type=MESH,
        )

    sends = []
    for off in list(range(1, chips)) + [0]:
        for i in (1, 2, 0):
            if off == 0:
                copy = remote(i, 0, sources[i], me, sibling, fsend_sem, frecv_sem)
            else:
                copy = remote(i, off, sources[i], me, peer(off), send_sem, recv_sem)
            copy.start()
            sends.append(copy)
    own = []
    for i in range(3):
        copy = pltpu.make_async_copy(sources[i], places[i].at[me], own_sem.at[i])
        copy.start()
        own.append(copy)

    tokens = q_ref.shape[1]
    group_size = q_ref.shape[2] // HD
    rows = tokens * group_size
    q = stack_heads(q_ref[0], group_size)
    fresh = fk_ref.shape[1] * fk_ref.shape[2]
    fk = fk_ref[0].reshape(fresh, HD)
    fv_t = fv_ref[0].reshape(fresh, HD).T
    fv_t = jnp.concatenate([fv_t, jnp.ones((ONES, fresh), jnp.bfloat16)], axis=0)
    sv_t = sv_ref[0].astype(jnp.float32).T.astype(jnp.bfloat16)
    sv_t = jnp.concatenate([sv_t, jnp.ones((ONES, tokens), jnp.bfloat16)], axis=0)
    for lo in range(0, rows, CHUNK):
        block = q[lo : lo + CHUNK]
        fs = nt_dot(fk, block)
        ss = nt_dot(sk_ref[0], block)
        key_at = lax.broadcasted_iota(jnp.int32, (tokens, CHUNK), 0)
        token_at = (lax.broadcasted_iota(jnp.int32, (tokens, CHUNK), 1) + lo) % tokens
        ss = jnp.where(key_at <= token_at, ss, very_low)
        top = jnp.maximum(
            jnp.max(fs, axis=0, keepdims=True), jnp.max(ss, axis=0, keepdims=True)
        )
        fw = jnp.exp2((fs - top) * FACTOR).astype(jnp.bfloat16)
        sw = jnp.exp2((ss - top) * FACTOR).astype(jnp.bfloat16)
        host_acc[:, lo : lo + CHUNK] = nn_dot(fv_t, fw) + nn_dot(sv_t, sw)
        host_max[:, lo : lo + CHUNK] = jnp.broadcast_to(top, (8, CHUNK))

    for off in range(1, chips):
        slot = origin(off, core)
        for i in (1, 2, 0):
            remote(i, off, sources[i], slot, peer(off), send_sem, recv_sem).wait_recv()
            copy = remote(i, off, places[i].at[slot], slot, sibling, fsend_sem, frecv_sem)
            copy.start()
            sends.append(copy)
    for off in range(chips):
        slot = origin(off, 1 - core)
        for i in range(3):
            remote(i, off, sources[i], slot, sibling, fsend_sem, frecv_sem).wait_recv()
    for copy in own:
        copy.wait()
    for copy in sends:
        copy.wait_send()


def slot_kernel(cites, q_all, sel_all, k_ref, v_ref, out_ref, stat_ref, v_t, acc, top):
    me = lax.axis_index("pass")
    total, tokens, width = q_all.shape
    group_size = width // HD
    rows = tokens * group_size
    local, length, _ = k_ref.shape
    cite_count = sel_all.shape[1]
    picks = sel_all.shape[2]
    for p in range(local):
        v_t[p, 0:HD, :] = v_ref[p].T
        v_t[p, HD:, :] = jnp.ones((ONES, length), jnp.bfloat16)

    def one_request(r, carry):
        acc[...] = jnp.zeros_like(acc)
        top[...] = jnp.full_like(top, very_low)

        def one_cite(c, inner):
            cited = cites[r, 0, c]

            @pl.when(cited // local == me)
            def _():
                p = cited % local
                picked = sel_all[r, pl.ds(c, 1), :]
                at = lax.broadcasted_iota(jnp.int32, (length, picks), 0)
                bias = jnp.where(at == picked, very_low, 0.0).astype(jnp.bfloat16)
                keys = jnp.concatenate([k_ref[p], bias], axis=1)
                q = stack_heads(q_all[r], group_size)
                q = jnp.concatenate([q, jnp.ones((rows, picks), jnp.bfloat16)], axis=1)
                values = v_t[p]
                for lo in range(0, rows, CHUNK):
                    s = nt_dot(keys, q[lo : lo + CHUNK])
                    old = top[0:1, lo : lo + CHUNK]
                    new = jnp.maximum(old, jnp.max(s, axis=0, keepdims=True))
                    w = jnp.exp2((s - new) * FACTOR).astype(jnp.bfloat16)
                    scale = jnp.exp2((old - new) * FACTOR)
                    acc[:, lo : lo + CHUNK] = acc[:, lo : lo + CHUNK] * scale + nn_dot(values, w)
                    top[:, lo : lo + CHUNK] = jnp.broadcast_to(new, (8, CHUNK))

            return inner

        lax.fori_loop(0, cite_count, one_cite, 0)
        weight = acc[HD : HD + 8, :]
        out_ref[r] = (acc[0:HD, :] / jnp.maximum(weight[0:1], 1.0)).astype(jnp.bfloat16)
        stat_ref[r, 0:8, :] = top[...]
        stat_ref[r, 8:16, :] = weight
        return carry

    lax.fori_loop(0, total, one_request, 0)


def merge_kernel(
    n,
    kv,
    out_all,
    stat_all,
    host_acc,
    host_max,
    result,
    got_out,
    got_stat,
    kv_send,
    kv_recv,
    own_sem,
    send_sem,
    recv_sem,
    kv_send_sem,
    kv_recv_sem,
):
    me = lax.axis_index("pass")
    my_kv = lax.axis_index("kv")
    rows = host_max.shape[1]
    part, group_size = kv_send.shape[1], kv_send.shape[2] // HD
    tokens = part * kv
    barrier = pltpu.get_barrier_semaphore()
    for off in range(1, n):
        pl.semaphore_signal(
            barrier, inc=1, device_id={"pass": (me + off) % n}, device_id_type=MESH
        )
    for off in range(1, kv):
        pl.semaphore_signal(
            barrier, inc=1, device_id={"kv": (my_kv + off) % kv}, device_id_type=MESH
        )
    pl.semaphore_wait(barrier, n + kv - 2)

    def remote(i, off, target, slot):
        source, place = ((out_all, got_out), (stat_all, got_stat))[i]
        return pltpu.make_async_remote_copy(
            src_ref=source.at[target],
            dst_ref=place.at[slot],
            send_sem=send_sem.at[i, off],
            recv_sem=recv_sem.at[i, off],
            device_id={"pass": target},
            device_id_type=MESH,
        )

    sends = []
    for off in range(1, n):
        for i in (1, 0):
            copy = remote(i, off, (me + off) % n, me)
            copy.start()
            sends.append(copy)
    own = []
    for i, (source, place) in enumerate(((out_all, got_out), (stat_all, got_stat))):
        copy = pltpu.make_async_copy(source.at[me], place.at[me], own_sem.at[i])
        copy.start()
        own.append(copy)
    for copy in own:
        copy.wait()
    for off in range(1, n):
        for i in (1, 0):
            remote(i, off, (me + off) % n, (me + n - off) % n).wait_recv()

    top = host_max[0:1, :]
    ceiling = top
    for i in range(n):
        ceiling = jnp.maximum(ceiling, got_stat[i, 0:1, :])
    near = jnp.exp2((top - ceiling) * FACTOR)
    numer = host_acc[0:HD, :] * near
    denom = host_acc[HD : HD + 1, :] * near
    for i in range(n):
        share = got_stat[i, 8:9, :] * jnp.exp2((got_stat[i, 0:1, :] - ceiling) * FACTOR)
        numer = numer + got_out[i].astype(jnp.float32) * share
        denom = denom + share
    done = (numer / denom).T
    for j in range(kv):
        block = [
            done[g * tokens + j * part : g * tokens + (j + 1) * part] for g in range(group_size)
        ]
        kv_send[j] = jnp.concatenate(block, axis=1).astype(jnp.bfloat16)

    def across(off, target, slot):
        return pltpu.make_async_remote_copy(
            src_ref=kv_send.at[target],
            dst_ref=kv_recv.at[slot],
            send_sem=kv_send_sem.at[off],
            recv_sem=kv_recv_sem.at[off],
            device_id={"kv": target},
            device_id_type=MESH,
        )

    for off in range(1, kv):
        copy = across(off, (my_kv + off) % kv, my_kv)
        copy.start()
        sends.append(copy)
    kv_recv[my_kv] = kv_send[my_kv]
    for off in range(1, kv):
        across(off, (my_kv + off) % kv, (my_kv + kv - off) % kv).wait_recv()
    width = kv_send.shape[2]
    for i in range(kv):
        result[0, :, i * width : (i + 1) * width] = kv_recv[i]
    for copy in sends:
        copy.wait_send()


VM = pl.BlockSpec(memory_space=pltpu.VMEM)
ANY = pl.BlockSpec(memory_space=pl.ANY)
SM = pl.BlockSpec(memory_space=pltpu.SMEM)
LIMIT = 48 * 1024 * 1024


def body(
    n,
    kv,
    queries,
    suffix_keys,
    suffix_values,
    passage_keys,
    passage_values,
    fresh_keys,
    fresh_values,
    citations,
    selected,
):
    _, tokens, width = queries.shape
    rows = tokens * width // HD
    local, length, _ = passage_keys.shape
    _, cite_count, picks = selected.shape
    chips = n // 2
    bf, f32, i32 = jnp.bfloat16, jnp.float32, jnp.int32
    dma = pltpu.SemaphoreType.DMA
    q_all, cite_all, sel_all, host_acc, host_max = pl.pallas_call(
        functools.partial(gather_kernel, n),
        out_shape=(
            jax.ShapeDtypeStruct((n, tokens, width), bf),
            jax.ShapeDtypeStruct((n, 8, 128), i32),
            jax.ShapeDtypeStruct((n, cite_count, picks), i32),
            jax.ShapeDtypeStruct((HD + ONES, rows), f32),
            jax.ShapeDtypeStruct((8, rows), f32),
        ),
        in_specs=[VM] * 7,
        out_specs=(ANY, ANY, ANY, VM, VM),
        scratch_shapes=[
            pltpu.VMEM((8, 128), i32),
            dma((3,)),
            dma((3, chips)),
            dma((3, chips)),
            dma((3, chips)),
            dma((3, chips)),
        ],
        compiler_params=pltpu.CompilerParams(
            collective_id=0, has_side_effects=True, vmem_limit_bytes=LIMIT
        ),
        name="gather_queries",
    )(queries, suffix_keys, suffix_values, fresh_keys, fresh_values, citations, selected)

    out_all, stat_all = pl.pallas_call(
        slot_kernel,
        out_shape=(
            jax.ShapeDtypeStruct((n, HD, rows), bf),
            jax.ShapeDtypeStruct((n, 16, rows), f32),
        ),
        in_specs=[SM, VM, VM, VM, VM],
        out_specs=(VM, VM),
        scratch_shapes=[
            pltpu.VMEM((local, HD + ONES, length), bf),
            pltpu.VMEM((HD + ONES, rows), f32),
            pltpu.VMEM((8, rows), f32),
        ],
        compiler_params=pltpu.CompilerParams(vmem_limit_bytes=LIMIT),
        name="passage_slots",
    )(cite_all, q_all, sel_all, passage_keys, passage_values)

    return pl.pallas_call(
        functools.partial(merge_kernel, n, kv),
        out_shape=jax.ShapeDtypeStruct((1, tokens // kv, width * kv), bf),
        in_specs=[ANY, ANY, VM, VM],
        out_specs=VM,
        scratch_shapes=[
            pltpu.VMEM((n, HD, rows), bf),
            pltpu.VMEM((n, 16, rows), f32),
            pltpu.VMEM((kv, tokens // kv, width), bf),
            pltpu.VMEM((kv, tokens // kv, width), bf),
            dma((2,)),
            dma((2, n)),
            dma((2, n)),
            dma((kv,)),
            dma((kv,)),
        ],
        compiler_params=pltpu.CompilerParams(
            collective_id=1, has_side_effects=True, vmem_limit_bytes=LIMIT
        ),
        name="merge_groups",
    )(out_all, stat_all, host_acc, host_max)


def solution(mesh):
    placed = (
        P("pass", None, "kv"),
        P("pass", None, "kv"),
        P("pass", None, "kv"),
        P("pass", None, "kv"),
        P("pass", None, "kv"),
        P("pass", None, None, "kv"),
        P("pass", None, None, "kv"),
        P("pass", None),
        P("pass", None, None),
    )
    return jax.shard_map(
        functools.partial(body, mesh.shape["pass"], mesh.shape["kv"]),
        mesh=mesh,
        in_specs=placed,
        out_specs=P("pass", "kv", None),
        check_vma=False,
    )
```

```python
import functools
import math

import jax
import jax.numpy as jnp
from jax import lax
from jax.experimental import pallas as pl
from jax.experimental.pallas import tpu as pltpu
from jax.sharding import PartitionSpec as P

HD = 128
MESH = pl.DeviceIdType.MESH
very_low = -1e30
FACTOR = math.log2(math.e) / math.sqrt(HD)
ONES = 16
CHUNK = 256


def nt_dot(a, b):
    return lax.dot_general(a, b, (((1,), (1,)), ((), ())), preferred_element_type=jnp.float32)


def nn_dot(a, b):
    return jnp.dot(a, b, preferred_element_type=jnp.float32)


def stack_heads(rows, group_size):
    return jnp.concatenate([rows[:, g * HD : (g + 1) * HD] for g in range(group_size)], axis=0)


def gather_kernel(
    n,
    q_ref,
    sk_ref,
    sv_ref,
    fk_ref,
    fv_ref,
    cite_ref,
    sel_ref,
    q_all,
    cite_all,
    sel_all,
    host_acc,
    host_max,
    cite_buf,
    cite_in,
    q_buf,
    sk_buf,
    sv_buf,
    fk_buf,
    fv_buf,
    in_sem,
    own_sem,
    send_sem,
    recv_sem,
    fsend_sem,
    frecv_sem,
):
    loads = [pltpu.make_async_copy(cite_ref, cite_in, in_sem.at[5])]
    for i, (source, place) in enumerate(
        ((q_ref, q_buf), (sk_ref, sk_buf), (fk_ref, fk_buf), (fv_ref, fv_buf), (sv_ref, sv_buf))
    ):
        loads.append(pltpu.make_async_copy(source, place, in_sem.at[i]))
    for copy in loads:
        copy.start()
    me = lax.axis_index("pass")
    chip, core = me // 2, me % 2
    chips = n // 2
    sibling = chip * 2 + (1 - core)

    def peer(off):
        return ((chip + off) % chips) * 2 + core

    def origin(off, lane):
        return ((chip + chips - off) % chips) * 2 + lane

    barrier = pltpu.get_barrier_semaphore()
    for target in [sibling] + [peer(off) for off in range(1, chips)]:
        pl.semaphore_signal(barrier, inc=1, device_id={"pass": target}, device_id_type=MESH)
    cite_buf[...] = jnp.zeros_like(cite_buf)
    loads[0].wait()
    cite_buf[0:1, 0 : cite_ref.shape[1]] = cite_in[...]
    pl.semaphore_wait(barrier, chips)

    sources = (q_ref.at[0], cite_buf, sel_ref.at[0])
    places = (q_all, cite_all, sel_all)

    def remote(i, off, source, slot, target, send, recv):
        return pltpu.make_async_remote_copy(
            src_ref=source,
            dst_ref=places[i].at[slot],
            send_sem=send.at[i, off],
            recv_sem=recv.at[i, off],
            device_id={"pass": target},
            device_id_type=MESH,
        )

    sends = []
    for off in list(range(1, chips)) + [0]:
        for i in (1, 2, 0):
            if off == 0:
                copy = remote(i, 0, sources[i], me, sibling, fsend_sem, frecv_sem)
            else:
                copy = remote(i, off, sources[i], me, peer(off), send_sem, recv_sem)
            copy.start()
            sends.append(copy)
    own = []
    for i in range(3):
        copy = pltpu.make_async_copy(sources[i], places[i].at[me], own_sem.at[i])
        copy.start()
        own.append(copy)

    for copy in loads[1:]:
        copy.wait()
    tokens = q_ref.shape[1]
    group_size = q_ref.shape[2] // HD
    rows = tokens * group_size
    q = stack_heads(q_buf[0], group_size)
    fresh = fk_ref.shape[1] * fk_ref.shape[2]
    fk = fk_buf[0].reshape(fresh, HD)
    fv_t = fv_buf[0].reshape(fresh, HD).T
    fv_t = jnp.concatenate([fv_t, jnp.ones((ONES, fresh), jnp.bfloat16)], axis=0)
    sv_t = sv_buf[0].astype(jnp.float32).T.astype(jnp.bfloat16)
    sv_t = jnp.concatenate([sv_t, jnp.ones((ONES, tokens), jnp.bfloat16)], axis=0)
    for lo in range(0, rows, CHUNK):
        block = q[lo : lo + CHUNK]
        fs = nt_dot(fk, block)
        ss = nt_dot(sk_buf[0], block)
        key_at = lax.broadcasted_iota(jnp.int32, (tokens, CHUNK), 0)
        token_at = (lax.broadcasted_iota(jnp.int32, (tokens, CHUNK), 1) + lo) % tokens
        ss = jnp.where(key_at <= token_at, ss, very_low)
        top = jnp.maximum(
            jnp.max(fs, axis=0, keepdims=True), jnp.max(ss, axis=0, keepdims=True)
        )
        fw = jnp.exp2((fs - top) * FACTOR).astype(jnp.bfloat16)
        sw = jnp.exp2((ss - top) * FACTOR).astype(jnp.bfloat16)
        host_acc[:, lo : lo + CHUNK] = nn_dot(fv_t, fw) + nn_dot(sv_t, sw)
        host_max[:, lo : lo + CHUNK] = jnp.broadcast_to(top, (8, CHUNK))

    for off in range(1, chips):
        slot = origin(off, core)
        for i in (1, 2, 0):
            remote(i, off, sources[i], slot, peer(off), send_sem, recv_sem).wait_recv()
            copy = remote(i, off, places[i].at[slot], slot, sibling, fsend_sem, frecv_sem)
            copy.start()
            sends.append(copy)
    for off in range(chips):
        slot = origin(off, 1 - core)
        for i in range(3):
            remote(i, off, sources[i], slot, sibling, fsend_sem, frecv_sem).wait_recv()
    for copy in own:
        copy.wait()
    for copy in sends:
        copy.wait_send()


def slot_kernel(
    cites,
    q_hbm,
    sel_hbm,
    k_hbm,
    v_hbm,
    out_ref,
    stat_ref,
    q_all,
    sel_all,
    k_ref,
    v_ref,
    v_t,
    acc,
    top,
    peak,
    bias,
    first,
    second,
    live,
    in_sem,
):
    me = lax.axis_index("pass")
    total, tokens, width = q_all.shape
    group_size = width // HD
    rows = tokens * group_size
    half = rows // 2
    heads_half = group_size // 2
    local, length, _ = k_ref.shape
    cite_count = sel_all.shape[1]
    picks = sel_all.shape[2]
    loads = []
    for i, (source, place) in enumerate(
        ((v_hbm, v_ref), (sel_hbm, sel_all), (k_hbm, k_ref), (q_hbm, q_all))
    ):
        copy = pltpu.make_async_copy(source, place, in_sem.at[i])
        copy.start()
        loads.append(copy)

    def collect(i, count):
        live[count] = i
        cited = cites[i // cite_count, 0, i % cite_count]
        return count + (cited // local == me).astype(jnp.int32)

    count = lax.fori_loop(0, total * cite_count, collect, 0)
    acc[...] = jnp.zeros_like(acc)
    top[...] = jnp.full_like(top, very_low)
    loads[0].wait()
    for p in range(local):
        v_t[p, 0:HD, :] = v_ref[p].T
        v_t[p, HD:, :] = jnp.ones((ONES, length), jnp.bfloat16)
    for copy in loads[1:]:
        copy.wait()

    def where(i):
        at = live[jnp.minimum(i, jnp.maximum(count - 1, 0))]
        r, c = at // cite_count, at % cite_count
        return r, c, cites[r, 0, c] % local

    def fill_bias(r, c):
        at = lax.broadcasted_iota(jnp.int32, (length, picks), 0)
        picked = sel_all[r, pl.ds(c, 1), :]
        bias[...] = jnp.where(at == picked, very_low, 0.0).astype(jnp.bfloat16)

    def score(r, p, side, place):
        keys = jnp.concatenate([k_ref[p], bias[...]], axis=1)
        cut = heads_half * HD
        q = stack_heads(q_all[r, :, side * cut : (side + 1) * cut], heads_half)
        q = jnp.concatenate([q, jnp.ones((half, picks), jnp.bfloat16)], axis=1)
        s = nt_dot(keys, q)
        place[...] = s
        peak[side] = jnp.broadcast_to(jnp.max(s, axis=0, keepdims=True), (8, half))

    def weigh(r, p, side, place):
        lo, hi = side * half, (side + 1) * half
        old = top[r, 0:1, lo:hi]
        new = jnp.maximum(old, peak[side, 0:1, :])
        w = jnp.exp2((place[...] - new) * FACTOR).astype(jnp.bfloat16)
        scale = jnp.exp2((old - new) * FACTOR)
        acc[r, :, lo:hi] = acc[r, :, lo:hi] * scale + nn_dot(v_t[p], w)
        top[r, :, lo:hi] = jnp.broadcast_to(new, (8, half))

    r, c, p = where(0)
    fill_bias(r, c)
    score(r, p, 0, first)

    def one_slot(i, carry):
        r, c, p = where(i)
        score(r, p, 1, second)
        weigh(r, p, 0, first)
        r_next, c_next, p_next = where(i + 1)
        fill_bias(r_next, c_next)
        score(r_next, p_next, 0, first)
        weigh(r, p, 1, second)
        return carry

    lax.fori_loop(0, count, one_slot, 0)

    def finish(r, carry):
        weight = acc[r, HD : HD + 8, :]
        out_ref[r] = (acc[r, 0:HD, :] / jnp.maximum(weight[0:1], 1.0)).astype(jnp.bfloat16)
        stat_ref[r, 0:8, :] = top[r]
        stat_ref[r, 8:16, :] = weight
        return carry

    lax.fori_loop(0, total, finish, 0)


def merge_kernel(
    n,
    kv,
    out_all,
    stat_all,
    host_acc,
    host_max,
    result,
    got_out,
    got_stat,
    kv_send,
    kv_recv,
    own_sem,
    send_sem,
    recv_sem,
    kv_send_sem,
    kv_recv_sem,
):
    me = lax.axis_index("pass")
    my_kv = lax.axis_index("kv")
    rows = host_max.shape[1]
    part, group_size = kv_send.shape[1], kv_send.shape[2] // HD
    tokens = part * kv
    barrier = pltpu.get_barrier_semaphore()
    for off in range(1, n):
        pl.semaphore_signal(
            barrier, inc=1, device_id={"pass": (me + off) % n}, device_id_type=MESH
        )
    for off in range(1, kv):
        pl.semaphore_signal(
            barrier, inc=1, device_id={"kv": (my_kv + off) % kv}, device_id_type=MESH
        )
    pl.semaphore_wait(barrier, n + kv - 2)

    def remote(i, off, target, slot):
        source, place = ((out_all, got_out), (stat_all, got_stat))[i]
        return pltpu.make_async_remote_copy(
            src_ref=source.at[target],
            dst_ref=place.at[slot],
            send_sem=send_sem.at[i, off],
            recv_sem=recv_sem.at[i, off],
            device_id={"pass": target},
            device_id_type=MESH,
        )

    sends = []
    for off in range(1, n):
        for i in (1, 0):
            copy = remote(i, off, (me + off) % n, me)
            copy.start()
            sends.append(copy)
    own = []
    for i, (source, place) in enumerate(((out_all, got_out), (stat_all, got_stat))):
        copy = pltpu.make_async_copy(source.at[me], place.at[me], own_sem.at[i])
        copy.start()
        own.append(copy)
    for copy in own:
        copy.wait()
    for off in range(1, n):
        for i in (1, 0):
            remote(i, off, (me + off) % n, (me + n - off) % n).wait_recv()

    top = host_max[0:1, :]
    ceiling = top
    for i in range(n):
        ceiling = jnp.maximum(ceiling, got_stat[i, 0:1, :])
    near = jnp.exp2((top - ceiling) * FACTOR)
    numer = host_acc[0:HD, :] * near
    denom = host_acc[HD : HD + 1, :] * near
    for i in range(n):
        share = got_stat[i, 8:9, :] * jnp.exp2((got_stat[i, 0:1, :] - ceiling) * FACTOR)
        numer = numer + got_out[i].astype(jnp.float32) * share
        denom = denom + share
    done = (numer / denom).T
    for j in range(kv):
        block = [
            done[g * tokens + j * part : g * tokens + (j + 1) * part] for g in range(group_size)
        ]
        kv_send[j] = jnp.concatenate(block, axis=1).astype(jnp.bfloat16)

    def across(off, target, slot):
        return pltpu.make_async_remote_copy(
            src_ref=kv_send.at[target],
            dst_ref=kv_recv.at[slot],
            send_sem=kv_send_sem.at[off],
            recv_sem=kv_recv_sem.at[off],
            device_id={"kv": target},
            device_id_type=MESH,
        )

    for off in range(1, kv):
        copy = across(off, (my_kv + off) % kv, my_kv)
        copy.start()
        sends.append(copy)
    kv_recv[my_kv] = kv_send[my_kv]
    for off in range(1, kv):
        across(off, (my_kv + off) % kv, (my_kv + kv - off) % kv).wait_recv()
    width = kv_send.shape[2]
    for i in range(kv):
        result[0, :, i * width : (i + 1) * width] = kv_recv[i]
    for copy in sends:
        copy.wait_send()


VM = pl.BlockSpec(memory_space=pltpu.VMEM)
ANY = pl.BlockSpec(memory_space=pl.ANY)
SM = pl.BlockSpec(memory_space=pltpu.SMEM)
LIMIT = 62 * 1024 * 1024


def body(
    n,
    kv,
    queries,
    suffix_keys,
    suffix_values,
    passage_keys,
    passage_values,
    fresh_keys,
    fresh_values,
    citations,
    selected,
):
    _, tokens, width = queries.shape
    rows = tokens * width // HD
    local, length, _ = passage_keys.shape
    _, cite_count, picks = selected.shape
    chips = n // 2
    bf, f32, i32 = jnp.bfloat16, jnp.float32, jnp.int32
    dma = pltpu.SemaphoreType.DMA
    q_all, cite_all, sel_all, host_acc, host_max = pl.pallas_call(
        functools.partial(gather_kernel, n),
        out_shape=(
            jax.ShapeDtypeStruct((n, tokens, width), bf),
            jax.ShapeDtypeStruct((n, 8, 128), i32),
            jax.ShapeDtypeStruct((n, cite_count, picks), i32),
            jax.ShapeDtypeStruct((HD + ONES, rows), f32),
            jax.ShapeDtypeStruct((8, rows), f32),
        ),
        in_specs=[ANY] * 7,
        out_specs=(ANY, ANY, ANY, VM, VM),
        scratch_shapes=[
            pltpu.VMEM((8, 128), i32),
            pltpu.VMEM(citations.shape, i32),
            pltpu.VMEM(queries.shape, bf),
            pltpu.VMEM(suffix_keys.shape, bf),
            pltpu.VMEM(suffix_values.shape, bf),
            pltpu.VMEM(fresh_keys.shape, bf),
            pltpu.VMEM(fresh_values.shape, bf),
            dma((6,)),
            dma((3,)),
            dma((3, chips)),
            dma((3, chips)),
            dma((3, chips)),
            dma((3, chips)),
        ],
        compiler_params=pltpu.CompilerParams(
            collective_id=0, has_side_effects=True, vmem_limit_bytes=LIMIT
        ),
        name="gather_queries",
    )(queries, suffix_keys, suffix_values, fresh_keys, fresh_values, citations, selected)

    out_all, stat_all = pl.pallas_call(
        slot_kernel,
        out_shape=(
            jax.ShapeDtypeStruct((n, HD, rows), bf),
            jax.ShapeDtypeStruct((n, 16, rows), f32),
        ),
        in_specs=[SM, ANY, ANY, ANY, ANY],
        out_specs=(VM, VM),
        scratch_shapes=[
            pltpu.VMEM((n, tokens, width), bf),
            pltpu.VMEM((n, cite_count, picks), i32),
            pltpu.VMEM(passage_keys.shape, bf),
            pltpu.VMEM(passage_values.shape, bf),
            pltpu.VMEM((local, HD + ONES, length), bf),
            pltpu.VMEM((n, HD + ONES, rows), f32),
            pltpu.VMEM((n, 8, rows), f32),
            pltpu.VMEM((2, 8, rows // 2), f32),
            pltpu.VMEM((length, picks), bf),
            pltpu.VMEM((length, rows // 2), f32),
            pltpu.VMEM((length, rows // 2), f32),
            pltpu.SMEM((n * cite_count + 1,), i32),
            dma((4,)),
        ],
        compiler_params=pltpu.CompilerParams(vmem_limit_bytes=LIMIT),
        name="passage_slots",
    )(cite_all, q_all, sel_all, passage_keys, passage_values)

    return pl.pallas_call(
        functools.partial(merge_kernel, n, kv),
        out_shape=jax.ShapeDtypeStruct((1, tokens // kv, width * kv), bf),
        in_specs=[ANY, ANY, VM, VM],
        out_specs=VM,
        scratch_shapes=[
            pltpu.VMEM((n, HD, rows), bf),
            pltpu.VMEM((n, 16, rows), f32),
            pltpu.VMEM((kv, tokens // kv, width), bf),
            pltpu.VMEM((kv, tokens // kv, width), bf),
            dma((2,)),
            dma((2, n)),
            dma((2, n)),
            dma((kv,)),
            dma((kv,)),
        ],
        compiler_params=pltpu.CompilerParams(
            collective_id=1, has_side_effects=True, vmem_limit_bytes=LIMIT
        ),
        name="merge_groups",
    )(out_all, stat_all, host_acc, host_max)


def solution(mesh):
    placed = (
        P("pass", None, "kv"),
        P("pass", None, "kv"),
        P("pass", None, "kv"),
        P("pass", None, "kv"),
        P("pass", None, "kv"),
        P("pass", None, None, "kv"),
        P("pass", None, None, "kv"),
        P("pass", None),
        P("pass", None, None),
    )
    return jax.shard_map(
        functools.partial(body, mesh.shape["pass"], mesh.shape["kv"]),
        mesh=mesh,
        in_specs=placed,
        out_specs=P("pass", "kv", None),
        check_vma=False,
    )
```

```python
import functools
import math

import jax
import jax.numpy as jnp
from jax import lax
from jax.experimental import pallas as pl
from jax.experimental.pallas import tpu as pltpu
from jax.sharding import PartitionSpec as P

HD = 128
MESH = pl.DeviceIdType.MESH
very_low = -1e30
FACTOR = math.log2(math.e) / math.sqrt(HD)
ONES = 16
CHUNK = 256


def nt_dot(a, b):
    return lax.dot_general(a, b, (((1,), (1,)), ((), ())), preferred_element_type=jnp.float32)


def nn_dot(a, b):
    return jnp.dot(a, b, preferred_element_type=jnp.float32)


def stack_heads(rows, group_size):
    return jnp.concatenate([rows[:, g * HD : (g + 1) * HD] for g in range(group_size)], axis=0)


def gather_kernel(
    n,
    q_ref,
    sk_ref,
    sv_ref,
    fk_ref,
    fv_ref,
    cite_ref,
    sel_ref,
    q_all,
    cite_all,
    sel_all,
    host_acc,
    host_max,
    cite_buf,
    cite_in,
    q_buf,
    sk_buf,
    sv_buf,
    fk_buf,
    fv_buf,
    in_sem,
    own_sem,
    send_sem,
    recv_sem,
    fsend_sem,
    frecv_sem,
):
    loads = [pltpu.make_async_copy(cite_ref, cite_in, in_sem.at[5])]
    for i, (source, place) in enumerate(
        ((q_ref, q_buf), (sk_ref, sk_buf), (fk_ref, fk_buf), (fv_ref, fv_buf), (sv_ref, sv_buf))
    ):
        loads.append(pltpu.make_async_copy(source, place, in_sem.at[i]))
    for copy in loads:
        copy.start()
    me = lax.axis_index("pass")
    chip, core = me // 2, me % 2
    chips = n // 2
    sibling = chip * 2 + (1 - core)

    def peer(off):
        return ((chip + off) % chips) * 2 + core

    def origin(off, lane):
        return ((chip + chips - off) % chips) * 2 + lane

    barrier = pltpu.get_barrier_semaphore()
    for target in [sibling] + [peer(off) for off in range(1, chips)]:
        pl.semaphore_signal(barrier, inc=1, device_id={"pass": target}, device_id_type=MESH)
    cite_buf[...] = jnp.zeros_like(cite_buf)
    loads[0].wait()
    cite_buf[0:1, 0 : cite_ref.shape[1]] = cite_in[...]
    pl.semaphore_wait(barrier, chips)

    sources = (q_ref.at[0], cite_buf, sel_ref.at[0])
    places = (q_all, cite_all, sel_all)

    def remote(i, off, source, slot, target, send, recv):
        return pltpu.make_async_remote_copy(
            src_ref=source,
            dst_ref=places[i].at[slot],
            send_sem=send.at[i, off],
            recv_sem=recv.at[i, off],
            device_id={"pass": target},
            device_id_type=MESH,
        )

    sends = []
    for off in list(range(1, chips)) + [0]:
        for i in (1, 2, 0):
            if off == 0:
                copy = remote(i, 0, sources[i], me, sibling, fsend_sem, frecv_sem)
            else:
                copy = remote(i, off, sources[i], me, peer(off), send_sem, recv_sem)
            copy.start()
            sends.append(copy)
    own = []
    for i in range(3):
        copy = pltpu.make_async_copy(sources[i], places[i].at[me], own_sem.at[i])
        copy.start()
        own.append(copy)

    for copy in loads[1:]:
        copy.wait()
    tokens = q_ref.shape[1]
    group_size = q_ref.shape[2] // HD
    rows = tokens * group_size
    q = stack_heads(q_buf[0], group_size)
    fresh = fk_ref.shape[1] * fk_ref.shape[2]
    fk = fk_buf[0].reshape(fresh, HD)
    fv_t = fv_buf[0].reshape(fresh, HD).T
    fv_t = jnp.concatenate([fv_t, jnp.ones((ONES, fresh), jnp.bfloat16)], axis=0)
    sv_t = sv_buf[0].astype(jnp.float32).T.astype(jnp.bfloat16)
    sv_t = jnp.concatenate([sv_t, jnp.ones((ONES, tokens), jnp.bfloat16)], axis=0)
    for lo in range(0, rows, CHUNK):
        block = q[lo : lo + CHUNK]
        fs = nt_dot(fk, block)
        ss = nt_dot(sk_buf[0], block)
        key_at = lax.broadcasted_iota(jnp.int32, (tokens, CHUNK), 0)
        token_at = (lax.broadcasted_iota(jnp.int32, (tokens, CHUNK), 1) + lo) % tokens
        ss = jnp.where(key_at <= token_at, ss, very_low)
        top = jnp.maximum(
            jnp.max(fs, axis=0, keepdims=True), jnp.max(ss, axis=0, keepdims=True)
        )
        fw = jnp.exp2((fs - top) * FACTOR).astype(jnp.bfloat16)
        sw = jnp.exp2((ss - top) * FACTOR).astype(jnp.bfloat16)
        host_acc[:, lo : lo + CHUNK] = nn_dot(fv_t, fw) + nn_dot(sv_t, sw)
        host_max[:, lo : lo + CHUNK] = jnp.broadcast_to(top, (8, CHUNK))

    for off in range(1, chips):
        slot = origin(off, core)
        for i in (1, 2, 0):
            remote(i, off, sources[i], slot, peer(off), send_sem, recv_sem).wait_recv()
            copy = remote(i, off, places[i].at[slot], slot, sibling, fsend_sem, frecv_sem)
            copy.start()
            sends.append(copy)
    for off in range(chips):
        slot = origin(off, 1 - core)
        for i in range(3):
            remote(i, off, sources[i], slot, sibling, fsend_sem, frecv_sem).wait_recv()
    for copy in own:
        copy.wait()
    for copy in sends:
        copy.wait_send()


def slot_kernel(
    cites,
    q_hbm,
    sel_hbm,
    k_hbm,
    v_hbm,
    out_ref,
    stat_ref,
    q_all,
    sel_all,
    k_ref,
    v_ref,
    v_t,
    acc,
    top,
    peak,
    bias,
    first,
    second,
    live,
    in_sem,
):
    me = lax.axis_index("pass")
    total, tokens, width = q_all.shape
    group_size = width // HD
    rows = tokens * group_size
    half = rows // 2
    heads_half = group_size // 2
    local, length, _ = k_ref.shape
    cite_count = sel_all.shape[1]
    picks = sel_all.shape[2]
    loads = []
    for i, (source, place) in enumerate(
        ((v_hbm, v_ref), (sel_hbm, sel_all), (k_hbm, k_ref), (q_hbm, q_all))
    ):
        copy = pltpu.make_async_copy(source, place, in_sem.at[i])
        copy.start()
        loads.append(copy)

    def collect(i, count):
        live[count] = i
        cited = cites[i // cite_count, 0, i % cite_count]
        return count + (cited // local == me).astype(jnp.int32)

    count = lax.fori_loop(0, total * cite_count, collect, 0)
    acc[...] = jnp.zeros_like(acc)
    top[...] = jnp.full_like(top, very_low)
    loads[0].wait()
    for p in range(local):
        v_t[p, 0:HD, :] = v_ref[p].T
        v_t[p, HD:, :] = jnp.ones((ONES, length), jnp.bfloat16)
    for copy in loads[1:]:
        copy.wait()

    def where(i):
        at = live[jnp.minimum(i, jnp.maximum(count - 1, 0))]
        r, c = at // cite_count, at % cite_count
        return r, c, cites[r, 0, c] % local

    def fill_bias(r, c):
        at = lax.broadcasted_iota(jnp.int32, (length, picks), 0)
        picked = sel_all[r, pl.ds(c, 1), :]
        bias[...] = jnp.where(at == picked, very_low, 0.0).astype(jnp.bfloat16)

    def score(r, p, side, place):
        keys = jnp.concatenate([k_ref[p], bias[...]], axis=1)
        cut = heads_half * HD
        q = stack_heads(q_all[r, :, side * cut : (side + 1) * cut], heads_half)
        q = jnp.concatenate([q, jnp.ones((half, picks), jnp.bfloat16)], axis=1)
        s = nt_dot(keys, q)
        place[...] = s
        peak[side] = jnp.broadcast_to(jnp.max(s, axis=0, keepdims=True), (8, half))

    def weigh(r, p, side, place):
        lo, hi = side * half, (side + 1) * half
        old = top[r, 0:1, lo:hi]
        new = jnp.maximum(old, peak[side, 0:1, :])
        w = jnp.exp2((place[...] - new) * FACTOR).astype(jnp.bfloat16)
        scale = jnp.exp2((old - new) * FACTOR)
        acc[r, :, lo:hi] = acc[r, :, lo:hi] * scale + nn_dot(v_t[p], w)
        top[r, :, lo:hi] = jnp.broadcast_to(new, (8, half))

    r, c, p = where(0)
    fill_bias(r, c)
    score(r, p, 0, first)

    def one_slot(i, carry):
        r, c, p = where(i)
        score(r, p, 1, second)
        weigh(r, p, 0, first)
        r_next, c_next, p_next = where(i + 1)
        fill_bias(r_next, c_next)
        score(r_next, p_next, 0, first)
        weigh(r, p, 1, second)
        return carry

    lax.fori_loop(0, count, one_slot, 0)

    def finish(r, carry):
        weight = acc[r, HD : HD + 8, :]
        out = acc[r, 0:HD, :] * (1.0 / jnp.maximum(weight[0:1], 1.0))
        upper = lax.broadcasted_iota(jnp.int32, weight.shape, 0) < 4
        stat = jnp.where(upper, top[r], weight)
        for side in range(2):
            lo, hi = side * half, (side + 1) * half
            out_ref[r, side] = out[:, lo:hi].astype(jnp.bfloat16)
            stat_ref[r, side] = stat[:, lo:hi]
        return carry

    lax.fori_loop(0, total, finish, 0)


def merge_kernel(
    n,
    kv,
    out_all,
    stat_all,
    host_acc_hbm,
    host_max_hbm,
    result,
    host_acc,
    host_max,
    mine_out,
    mine_stat,
    pair_out,
    pair_stat,
    send_out,
    send_stat,
    got_out,
    got_stat,
    kv_send,
    kv_recv,
    host_sem,
    own_sem,
    pair_send_sem,
    pair_recv_sem,
    send_sem,
    recv_sem,
    kv_send_sem,
    kv_recv_sem,
):
    me = lax.axis_index("pass")
    my_kv = lax.axis_index("kv")
    chip, core = me // 2, me % 2
    chips = n // 2
    sibling = chip * 2 + (1 - core)
    pieces = out_all.shape[1]
    part, width = kv_send.shape[2:]
    heads = width // HD
    tokens = part * kv

    def target_chip(off):
        return (chip + off) % chips

    def source_chip(off):
        return (chip + chips - off) % chips

    barrier = pltpu.get_barrier_semaphore()
    for other in [sibling] + [target_chip(off) * 2 + core for off in range(1, chips)]:
        pl.semaphore_signal(barrier, inc=1, device_id={"pass": other}, device_id_type=MESH)
    for off in range(1, kv):
        pl.semaphore_signal(
            barrier, inc=1, device_id={"kv": (my_kv + off) % kv}, device_id_type=MESH
        )
    order = list(range(1, chips)) + [0]
    tables = ((out_all, mine_out, pair_out), (stat_all, mine_stat, pair_stat))
    own = {}
    for h in range(pieces):
        for off in order:
            for i, (source, place, _) in enumerate(tables):
                t = target_chip(off)
                own[h, off, i] = pltpu.make_async_copy(
                    source.at[t * 2 + core, h], place.at[off, h], own_sem.at[i, h, off]
                )
                own[h, off, i].start()
    loads = [
        pltpu.make_async_copy(host_acc_hbm, host_acc, host_sem.at[0]),
        pltpu.make_async_copy(host_max_hbm, host_max, host_sem.at[1]),
    ]
    for copy in loads:
        copy.start()
    pl.semaphore_wait(barrier, chips + kv - 1)

    def to_sibling(i, h, off):
        source, _, place = tables[i]
        return pltpu.make_async_remote_copy(
            src_ref=source.at[target_chip(off) * 2 + 1 - core, h],
            dst_ref=place.at[off, h],
            send_sem=pair_send_sem.at[i, h, off],
            recv_sem=pair_recv_sem.at[i, h, off],
            device_id={"pass": sibling},
            device_id_type=MESH,
        )

    def to_chip(i, h, off):
        source, place = ((send_out, got_out), (send_stat, got_stat))[i]
        return pltpu.make_async_remote_copy(
            src_ref=source.at[off, h],
            dst_ref=place.at[off, h],
            send_sem=send_sem.at[i, h, off],
            recv_sem=recv_sem.at[i, h, off],
            device_id={"pass": target_chip(off) * 2 + core},
            device_id_type=MESH,
        )

    def across(h, off, target, slot):
        return pltpu.make_async_remote_copy(
            src_ref=kv_send.at[h, target],
            dst_ref=kv_recv.at[h, slot],
            send_sem=kv_send_sem.at[h, off],
            recv_sem=kv_recv_sem.at[h, off],
            device_id={"kv": target},
            device_id_type=MESH,
        )

    sends = []
    for h in range(pieces):
        for off in order:
            for i in (1, 0):
                copy = to_sibling(i, h, off)
                copy.start()
                sends.append(copy)

    def pair_ready(h, off):
        for i in range(2):
            own[h, off, i].wait()
            to_sibling(i, h, off).wait_recv()

    def weighted(outs, stats):
        ceiling = stats[0][0]
        for top, _ in stats[1:]:
            ceiling = jnp.maximum(ceiling, top)
        numer, denom = 0.0, 0.0
        for out, (top, weight) in zip(outs, stats):
            scale = jnp.exp2((top - ceiling) * FACTOR)
            if weight is None:
                out, weight = out[0:HD], out[HD : HD + 1]
                numer = numer + out * scale
                denom = denom + weight * scale
            else:
                share = weight * scale
                numer = numer + out.astype(jnp.float32) * share
                denom = denom + share
        return ceiling, numer, denom

    def stats_of(ref, off, h):
        return ref[off, h, 0:1, :], ref[off, h, 4:5, :]

    for h in range(pieces):
        for off in range(1, chips):
            pair_ready(h, off)
            top, numer, denom = weighted(
                [mine_out[off, h], pair_out[off, h]],
                [stats_of(mine_stat, off, h), stats_of(pair_stat, off, h)],
            )
            send_out[off, h] = (numer / jnp.maximum(denom, 1.0)).astype(jnp.bfloat16)
            send_stat[off, h] = jnp.concatenate(
                [jnp.broadcast_to(top, (4, top.shape[1])), jnp.broadcast_to(denom, (4, top.shape[1]))]
            )
            for i in (1, 0):
                copy = to_chip(i, h, off)
                copy.start()
                sends.append(copy)
    for copy in loads:
        copy.wait()
    lanes = heads * tokens
    for h in range(pieces):
        pair_ready(h, 0)
        for off in range(1, chips):
            for i in range(2):
                to_chip(i, h, off).wait_recv()
        lo, hi = h * lanes, (h + 1) * lanes
        _, numer, denom = weighted(
            [host_acc[:, lo:hi], mine_out[0, h], pair_out[0, h]]
            + [got_out[off, h] for off in range(1, chips)],
            [(host_max[0:1, lo:hi], None), stats_of(mine_stat, 0, h), stats_of(pair_stat, 0, h)]
            + [stats_of(got_stat, off, h) for off in range(1, chips)],
        )
        done = (numer / denom).T
        for j in range(kv):
            block = [done[g * tokens + j * part : g * tokens + (j + 1) * part] for g in range(heads)]
            kv_send[h, j] = jnp.concatenate(block, axis=1).astype(jnp.bfloat16)
        for off in range(1, kv):
            copy = across(h, off, (my_kv + off) % kv, my_kv)
            copy.start()
            sends.append(copy)
        kv_recv[h, my_kv] = kv_send[h, my_kv]
    for h in range(pieces):
        for off in range(1, kv):
            across(h, off, (my_kv + off) % kv, (my_kv + kv - off) % kv).wait_recv()
        for i in range(kv):
            lo = (i * pieces + h) * heads * HD
            result[0, :, lo : lo + heads * HD] = kv_recv[h, i]
    for copy in sends:
        copy.wait_send()


VM = pl.BlockSpec(memory_space=pltpu.VMEM)
ANY = pl.BlockSpec(memory_space=pl.ANY)
SM = pl.BlockSpec(memory_space=pltpu.SMEM)
LIMIT = 62 * 1024 * 1024
MERGE_LIMIT = LIMIT


def body(
    n,
    kv,
    queries,
    suffix_keys,
    suffix_values,
    passage_keys,
    passage_values,
    fresh_keys,
    fresh_values,
    citations,
    selected,
):
    _, tokens, width = queries.shape
    rows = tokens * width // HD
    local, length, _ = passage_keys.shape
    _, cite_count, picks = selected.shape
    chips = n // 2
    bf, f32, i32 = jnp.bfloat16, jnp.float32, jnp.int32
    dma = pltpu.SemaphoreType.DMA
    q_all, cite_all, sel_all, host_acc, host_max = pl.pallas_call(
        functools.partial(gather_kernel, n),
        out_shape=(
            jax.ShapeDtypeStruct((n, tokens, width), bf),
            jax.ShapeDtypeStruct((n, 8, 128), i32),
            jax.ShapeDtypeStruct((n, cite_count, picks), i32),
            jax.ShapeDtypeStruct((HD + ONES, rows), f32),
            jax.ShapeDtypeStruct((8, rows), f32),
        ),
        in_specs=[ANY] * 7,
        out_specs=(ANY, ANY, ANY, VM, VM),
        scratch_shapes=[
            pltpu.VMEM((8, 128), i32),
            pltpu.VMEM(citations.shape, i32),
            pltpu.VMEM(queries.shape, bf),
            pltpu.VMEM(suffix_keys.shape, bf),
            pltpu.VMEM(suffix_values.shape, bf),
            pltpu.VMEM(fresh_keys.shape, bf),
            pltpu.VMEM(fresh_values.shape, bf),
            dma((6,)),
            dma((3,)),
            dma((3, chips)),
            dma((3, chips)),
            dma((3, chips)),
            dma((3, chips)),
        ],
        compiler_params=pltpu.CompilerParams(
            collective_id=0, has_side_effects=True, vmem_limit_bytes=LIMIT
        ),
        name="gather_queries",
    )(queries, suffix_keys, suffix_values, fresh_keys, fresh_values, citations, selected)

    out_all, stat_all = pl.pallas_call(
        slot_kernel,
        out_shape=(
            jax.ShapeDtypeStruct((n, 2, HD, rows // 2), bf),
            jax.ShapeDtypeStruct((n, 2, 8, rows // 2), f32),
        ),
        in_specs=[SM, ANY, ANY, ANY, ANY],
        out_specs=(VM, VM),
        scratch_shapes=[
            pltpu.VMEM((n, tokens, width), bf),
            pltpu.VMEM((n, cite_count, picks), i32),
            pltpu.VMEM(passage_keys.shape, bf),
            pltpu.VMEM(passage_values.shape, bf),
            pltpu.VMEM((local, HD + ONES, length), bf),
            pltpu.VMEM((n, HD + ONES, rows), f32),
            pltpu.VMEM((n, 8, rows), f32),
            pltpu.VMEM((2, 8, rows // 2), f32),
            pltpu.VMEM((length, picks), bf),
            pltpu.VMEM((length, rows // 2), f32),
            pltpu.VMEM((length, rows // 2), f32),
            pltpu.SMEM((n * cite_count + 1,), i32),
            dma((4,)),
        ],
        compiler_params=pltpu.CompilerParams(vmem_limit_bytes=LIMIT),
        name="passage_slots",
    )(cite_all, q_all, sel_all, passage_keys, passage_values)

    return pl.pallas_call(
        functools.partial(merge_kernel, n, kv),
        out_shape=jax.ShapeDtypeStruct((1, tokens // kv, width * kv), bf),
        in_specs=[ANY] * 4,
        out_specs=VM,
        scratch_shapes=[
            pltpu.VMEM((HD + ONES, rows), f32),
            pltpu.VMEM((8, rows), f32),
            *(
                [
                    pltpu.VMEM((chips, 2, HD, rows // 2), bf),
                    pltpu.VMEM((chips, 2, 8, rows // 2), f32),
                ]
                * 4
            ),
            pltpu.VMEM((2, kv, tokens // kv, width // 2), bf),
            pltpu.VMEM((2, kv, tokens // kv, width // 2), bf),
            dma((2,)),
            *([dma((2, 2, chips))] * 5),
            dma((2, kv)),
            dma((2, kv)),
        ],
        compiler_params=pltpu.CompilerParams(
            collective_id=1, has_side_effects=True, vmem_limit_bytes=MERGE_LIMIT
        ),
        name="merge_groups",
    )(out_all, stat_all, host_acc, host_max)


def solution(mesh):
    placed = (
        P("pass", None, "kv"),
        P("pass", None, "kv"),
        P("pass", None, "kv"),
        P("pass", None, "kv"),
        P("pass", None, "kv"),
        P("pass", None, None, "kv"),
        P("pass", None, None, "kv"),
        P("pass", None),
        P("pass", None, None),
    )
    return jax.shard_map(
        functools.partial(body, mesh.shape["pass"], mesh.shape["kv"]),
        mesh=mesh,
        in_specs=placed,
        out_specs=P("pass", "kv", None),
        check_vma=False,
    )
```

```python
import functools
import math

import jax
import jax.numpy as jnp
from jax import lax
from jax.experimental import pallas as pl
from jax.experimental.pallas import tpu as pltpu
from jax.sharding import PartitionSpec as P

HD = 128
MESH = pl.DeviceIdType.MESH
very_low = -1e30
FACTOR = math.log2(math.e) / math.sqrt(HD)
ONES = 16
CHUNK = 256
KEYS = 256


def nt_dot(a, b):
    return lax.dot_general(a, b, (((1,), (1,)), ((), ())), preferred_element_type=jnp.float32)


def nn_dot(a, b):
    return jnp.dot(a, b, preferred_element_type=jnp.float32)


def stack_heads(rows, group_size):
    return jnp.concatenate([rows[:, g * HD : (g + 1) * HD] for g in range(group_size)], axis=0)


def gather_kernel(
    n,
    q_ref,
    sk_ref,
    sv_ref,
    fk_ref,
    fv_ref,
    cite_ref,
    sel_ref,
    q_all,
    cite_all,
    sel_all,
    host_acc,
    host_max,
    cite_buf,
    cite_in,
    q_buf,
    sk_buf,
    sv_buf,
    fk_buf,
    fv_buf,
    in_sem,
    own_sem,
    send_sem,
    recv_sem,
    fsend_sem,
    frecv_sem,
):
    loads = [pltpu.make_async_copy(cite_ref, cite_in, in_sem.at[5])]
    for i, (source, place) in enumerate(
        ((q_ref, q_buf), (sk_ref, sk_buf), (fk_ref, fk_buf), (fv_ref, fv_buf), (sv_ref, sv_buf))
    ):
        loads.append(pltpu.make_async_copy(source, place, in_sem.at[i]))
    for copy in loads:
        copy.start()
    me = lax.axis_index("pass")
    chip, core = me // 2, me % 2
    chips = n // 2
    sibling = chip * 2 + (1 - core)

    def peer(off):
        return ((chip + off) % chips) * 2 + core

    def origin(off, lane):
        return ((chip + chips - off) % chips) * 2 + lane

    barrier = pltpu.get_barrier_semaphore()
    for target in [sibling] + [peer(off) for off in range(1, chips)]:
        pl.semaphore_signal(barrier, inc=1, device_id={"pass": target}, device_id_type=MESH)
    cite_buf[...] = jnp.zeros_like(cite_buf)
    loads[0].wait()
    cite_buf[0:1, 0 : cite_ref.shape[1]] = cite_in[...]
    pl.semaphore_wait(barrier, chips)

    sources = (q_ref.at[0], cite_buf, sel_ref.at[0])
    places = (q_all, cite_all, sel_all)

    def remote(i, off, source, slot, target, send, recv):
        return pltpu.make_async_remote_copy(
            src_ref=source,
            dst_ref=places[i].at[slot],
            send_sem=send.at[i, off],
            recv_sem=recv.at[i, off],
            device_id={"pass": target},
            device_id_type=MESH,
        )

    sends = []
    for off in list(range(1, chips)) + [0]:
        for i in (1, 2, 0):
            if off == 0:
                copy = remote(i, 0, sources[i], me, sibling, fsend_sem, frecv_sem)
            else:
                copy = remote(i, off, sources[i], me, peer(off), send_sem, recv_sem)
            copy.start()
            sends.append(copy)
    own = []
    for i in range(3):
        copy = pltpu.make_async_copy(sources[i], places[i].at[me], own_sem.at[i])
        copy.start()
        own.append(copy)

    for copy in loads[1:]:
        copy.wait()
    tokens = q_ref.shape[1]
    group_size = q_ref.shape[2] // HD
    rows = tokens * group_size
    q = stack_heads(q_buf[0], group_size)
    fresh = fk_ref.shape[1] * fk_ref.shape[2]
    fk = fk_buf[0].reshape(fresh, HD)
    fv_t = fv_buf[0].reshape(fresh, HD).T
    fv_t = jnp.concatenate([fv_t, jnp.ones((ONES, fresh), jnp.bfloat16)], axis=0)
    sv_t = sv_buf[0].astype(jnp.float32).T.astype(jnp.bfloat16)
    sv_t = jnp.concatenate([sv_t, jnp.ones((ONES, tokens), jnp.bfloat16)], axis=0)
    for lo in range(0, rows, CHUNK):
        block = q[lo : lo + CHUNK]
        fs = nt_dot(fk, block)
        ss = nt_dot(sk_buf[0], block)
        key_at = lax.broadcasted_iota(jnp.int32, (tokens, CHUNK), 0)
        token_at = (lax.broadcasted_iota(jnp.int32, (tokens, CHUNK), 1) + lo) % tokens
        ss = jnp.where(key_at <= token_at, ss, very_low)
        top = jnp.maximum(
            jnp.max(fs, axis=0, keepdims=True), jnp.max(ss, axis=0, keepdims=True)
        )
        fw = jnp.exp2((fs - top) * FACTOR).astype(jnp.bfloat16)
        sw = jnp.exp2((ss - top) * FACTOR).astype(jnp.bfloat16)
        host_acc[:, lo : lo + CHUNK] = nn_dot(fv_t, fw) + nn_dot(sv_t, sw)
        host_max[:, lo : lo + CHUNK] = jnp.broadcast_to(top, (8, CHUNK))

    for off in range(1, chips):
        slot = origin(off, core)
        for i in (1, 2, 0):
            remote(i, off, sources[i], slot, peer(off), send_sem, recv_sem).wait_recv()
            copy = remote(i, off, places[i].at[slot], slot, sibling, fsend_sem, frecv_sem)
            copy.start()
            sends.append(copy)
    for off in range(chips):
        slot = origin(off, 1 - core)
        for i in range(3):
            remote(i, off, sources[i], slot, sibling, fsend_sem, frecv_sem).wait_recv()
    for copy in own:
        copy.wait()
    for copy in sends:
        copy.wait_send()


def slot_kernel(
    cites,
    q_hbm,
    sel_hbm,
    k_hbm,
    v_hbm,
    out_ref,
    stat_ref,
    q_all,
    sel_all,
    k_ref,
    v_ref,
    v_t,
    acc,
    top,
    peak,
    bias,
    first,
    second,
    live,
    in_sem,
):
    me = lax.axis_index("pass")
    total, tokens, width = q_all.shape
    group_size = width // HD
    rows = tokens * group_size
    half = rows // 2
    heads_half = group_size // 2
    local, length, _ = k_ref.shape
    cite_count = sel_all.shape[1]
    picks = sel_all.shape[2]
    loads = []
    for i, (source, place) in enumerate(
        ((v_hbm, v_ref), (sel_hbm, sel_all), (k_hbm, k_ref), (q_hbm, q_all))
    ):
        copy = pltpu.make_async_copy(source, place, in_sem.at[i])
        copy.start()
        loads.append(copy)

    def collect(i, count):
        live[count] = i
        cited = cites[i // cite_count, 0, i % cite_count]
        return count + (cited // local == me).astype(jnp.int32)

    count = lax.fori_loop(0, total * cite_count, collect, 0)
    acc[...] = jnp.zeros_like(acc)
    top[...] = jnp.full_like(top, very_low)
    loads[0].wait()
    for p in range(local):
        v_t[p, 0:HD, :] = v_ref[p].T
        v_t[p, HD:, :] = jnp.ones((ONES, length), jnp.bfloat16)
    for copy in loads[1:]:
        copy.wait()

    def where(i):
        at = live[jnp.minimum(i, jnp.maximum(count - 1, 0))]
        r, c = at // cite_count, at % cite_count
        return r, c, cites[r, 0, c] % local

    def fill_bias(r, c):
        at = lax.broadcasted_iota(jnp.int32, (length, picks), 0)
        picked = sel_all[r, pl.ds(c, 1), :]
        bias[...] = jnp.where(at == picked, very_low, 0.0).astype(jnp.bfloat16)

    steps = [slice(lo, lo + KEYS) for lo in range(0, length, KEYS)]

    def score_steps(r, p, side, place):
        cut = heads_half * HD
        q = stack_heads(q_all[r, :, side * cut : (side + 1) * cut], heads_half)
        q = jnp.concatenate([q, jnp.ones((half, picks), jnp.bfloat16)], axis=1)
        highest = None
        for at in steps:
            keys = jnp.concatenate([k_ref[p, at, :], bias[at, :]], axis=1)
            s = nt_dot(keys, q)
            place[at, :] = s
            here = jnp.max(s.reshape(KEYS // 8, 8, half), axis=0)
            highest = here if highest is None else jnp.maximum(highest, here)
            yield
        peak[side] = jnp.broadcast_to(jnp.max(highest, axis=0, keepdims=True), (8, half))

    def weigh_steps(r, p, side, place):
        lo, hi = side * half, (side + 1) * half
        old = top[r, 0:1, lo:hi]
        new = jnp.maximum(old, peak[side, 0:1, :])
        scale = jnp.exp2((old - new) * FACTOR)
        top[r, :, lo:hi] = jnp.broadcast_to(new, (8, half))
        added = acc[r, :, lo:hi] * scale
        for at in steps:
            w = jnp.exp2((place[at, :] - new) * FACTOR).astype(jnp.bfloat16)
            added = added + nn_dot(v_t[p, :, at], w)
            yield
        acc[r, :, lo:hi] = added

    def together(*parts):
        waiting = list(parts)
        while waiting:
            waiting = [part for part in waiting if next(part, True) is None]

    r, c, p = where(0)
    fill_bias(r, c)
    together(score_steps(r, p, 0, first))

    def one_slot(i, carry):
        r, c, p = where(i)
        together(weigh_steps(r, p, 0, first), score_steps(r, p, 1, second))
        r_next, c_next, p_next = where(i + 1)
        fill_bias(r_next, c_next)
        together(weigh_steps(r, p, 1, second), score_steps(r_next, p_next, 0, first))
        return carry

    lax.fori_loop(0, count, one_slot, 0)

    def finish(r, carry):
        weight = acc[r, HD : HD + 8, :]
        out = acc[r, 0:HD, :] * (1.0 / jnp.maximum(weight[0:1], 1.0))
        upper = lax.broadcasted_iota(jnp.int32, weight.shape, 0) < 4
        stat = jnp.where(upper, top[r], weight)
        for side in range(2):
            lo, hi = side * half, (side + 1) * half
            out_ref[r, side] = out[:, lo:hi].astype(jnp.bfloat16)
            stat_ref[r, side] = stat[:, lo:hi]
        return carry

    lax.fori_loop(0, total, finish, 0)


def merge_kernel(
    n,
    kv,
    out_all,
    stat_all,
    host_acc_hbm,
    host_max_hbm,
    result,
    host_acc,
    host_max,
    mine_out,
    mine_stat,
    pair_out,
    pair_stat,
    send_out,
    send_stat,
    got_out,
    got_stat,
    kv_send,
    kv_recv,
    host_sem,
    own_sem,
    pair_send_sem,
    pair_recv_sem,
    send_sem,
    recv_sem,
    kv_send_sem,
    kv_recv_sem,
):
    me = lax.axis_index("pass")
    my_kv = lax.axis_index("kv")
    chip, core = me // 2, me % 2
    chips = n // 2
    sibling = chip * 2 + (1 - core)
    pieces = out_all.shape[1]
    part, width = kv_send.shape[2:]
    heads = width // HD
    tokens = part * kv

    def target_chip(off):
        return (chip + off) % chips

    def source_chip(off):
        return (chip + chips - off) % chips

    barrier = pltpu.get_barrier_semaphore()
    for other in [sibling] + [target_chip(off) * 2 + core for off in range(1, chips)]:
        pl.semaphore_signal(barrier, inc=1, device_id={"pass": other}, device_id_type=MESH)
    for off in range(1, kv):
        pl.semaphore_signal(
            barrier, inc=1, device_id={"kv": (my_kv + off) % kv}, device_id_type=MESH
        )
    order = list(range(1, chips)) + [0]
    tables = ((out_all, mine_out, pair_out), (stat_all, mine_stat, pair_stat))
    own = {}
    for h in range(pieces):
        for off in order:
            for i, (source, place, _) in enumerate(tables):
                t = target_chip(off)
                own[h, off, i] = pltpu.make_async_copy(
                    source.at[t * 2 + core, h], place.at[off, h], own_sem.at[i, h, off]
                )
                own[h, off, i].start()
    loads = [
        pltpu.make_async_copy(host_acc_hbm, host_acc, host_sem.at[0]),
        pltpu.make_async_copy(host_max_hbm, host_max, host_sem.at[1]),
    ]
    for copy in loads:
        copy.start()
    pl.semaphore_wait(barrier, chips + kv - 1)

    def to_sibling(i, h, off):
        source, _, place = tables[i]
        return pltpu.make_async_remote_copy(
            src_ref=source.at[target_chip(off) * 2 + 1 - core, h],
            dst_ref=place.at[off, h],
            send_sem=pair_send_sem.at[i, h, off],
            recv_sem=pair_recv_sem.at[i, h, off],
            device_id={"pass": sibling},
            device_id_type=MESH,
        )

    def to_chip(i, h, off):
        source, place = ((send_out, got_out), (send_stat, got_stat))[i]
        return pltpu.make_async_remote_copy(
            src_ref=source.at[off, h],
            dst_ref=place.at[off, h],
            send_sem=send_sem.at[i, h, off],
            recv_sem=recv_sem.at[i, h, off],
            device_id={"pass": target_chip(off) * 2 + core},
            device_id_type=MESH,
        )

    def across(h, off, target, slot):
        return pltpu.make_async_remote_copy(
            src_ref=kv_send.at[h, target],
            dst_ref=kv_recv.at[h, slot],
            send_sem=kv_send_sem.at[h, off],
            recv_sem=kv_recv_sem.at[h, off],
            device_id={"kv": target},
            device_id_type=MESH,
        )

    sends = []
    for h in range(pieces):
        for off in order:
            for i in (1, 0):
                copy = to_sibling(i, h, off)
                copy.start()
                sends.append(copy)

    def pair_ready(h, off):
        for i in range(2):
            own[h, off, i].wait()
            to_sibling(i, h, off).wait_recv()

    def weighted(outs, stats):
        ceiling = stats[0][0]
        for top, _ in stats[1:]:
            ceiling = jnp.maximum(ceiling, top)
        numer, denom = 0.0, 0.0
        for out, (top, weight) in zip(outs, stats):
            scale = jnp.exp2((top - ceiling) * FACTOR)
            if weight is None:
                out, weight = out[0:HD], out[HD : HD + 1]
                numer = numer + out * scale
                denom = denom + weight * scale
            else:
                share = weight * scale
                numer = numer + out.astype(jnp.float32) * share
                denom = denom + share
        return ceiling, numer, denom

    def stats_of(ref, off, h):
        return ref[off, h, 0:1, :], ref[off, h, 4:5, :]

    for h in range(pieces):
        for off in range(1, chips):
            pair_ready(h, off)
            top, numer, denom = weighted(
                [mine_out[off, h], pair_out[off, h]],
                [stats_of(mine_stat, off, h), stats_of(pair_stat, off, h)],
            )
            send_out[off, h] = (numer / jnp.maximum(denom, 1.0)).astype(jnp.bfloat16)
            send_stat[off, h] = jnp.concatenate(
                [jnp.broadcast_to(top, (4, top.shape[1])), jnp.broadcast_to(denom, (4, top.shape[1]))]
            )
            for i in (1, 0):
                copy = to_chip(i, h, off)
                copy.start()
                sends.append(copy)
    for copy in loads:
        copy.wait()
    lanes = heads * tokens
    for h in range(pieces):
        pair_ready(h, 0)
        for off in range(1, chips):
            for i in range(2):
                to_chip(i, h, off).wait_recv()
        lo, hi = h * lanes, (h + 1) * lanes
        _, numer, denom = weighted(
            [host_acc[:, lo:hi], mine_out[0, h], pair_out[0, h]]
            + [got_out[off, h] for off in range(1, chips)],
            [(host_max[0:1, lo:hi], None), stats_of(mine_stat, 0, h), stats_of(pair_stat, 0, h)]
            + [stats_of(got_stat, off, h) for off in range(1, chips)],
        )
        done = (numer / denom).T
        for j in range(kv):
            block = [done[g * tokens + j * part : g * tokens + (j + 1) * part] for g in range(heads)]
            kv_send[h, j] = jnp.concatenate(block, axis=1).astype(jnp.bfloat16)
        for off in range(1, kv):
            copy = across(h, off, (my_kv + off) % kv, my_kv)
            copy.start()
            sends.append(copy)
        kv_recv[h, my_kv] = kv_send[h, my_kv]
    for h in range(pieces):
        for off in range(1, kv):
            across(h, off, (my_kv + off) % kv, (my_kv + kv - off) % kv).wait_recv()
        for i in range(kv):
            lo = (i * pieces + h) * heads * HD
            result[0, :, lo : lo + heads * HD] = kv_recv[h, i]
    for copy in sends:
        copy.wait_send()


VM = pl.BlockSpec(memory_space=pltpu.VMEM)
ANY = pl.BlockSpec(memory_space=pl.ANY)
SM = pl.BlockSpec(memory_space=pltpu.SMEM)
LIMIT = 62 * 1024 * 1024
MERGE_LIMIT = LIMIT


def body(
    n,
    kv,
    queries,
    suffix_keys,
    suffix_values,
    passage_keys,
    passage_values,
    fresh_keys,
    fresh_values,
    citations,
    selected,
):
    _, tokens, width = queries.shape
    rows = tokens * width // HD
    local, length, _ = passage_keys.shape
    _, cite_count, picks = selected.shape
    chips = n // 2
    bf, f32, i32 = jnp.bfloat16, jnp.float32, jnp.int32
    dma = pltpu.SemaphoreType.DMA
    q_all, cite_all, sel_all, host_acc, host_max = pl.pallas_call(
        functools.partial(gather_kernel, n),
        out_shape=(
            jax.ShapeDtypeStruct((n, tokens, width), bf),
            jax.ShapeDtypeStruct((n, 8, 128), i32),
            jax.ShapeDtypeStruct((n, cite_count, picks), i32),
            jax.ShapeDtypeStruct((HD + ONES, rows), f32),
            jax.ShapeDtypeStruct((8, rows), f32),
        ),
        in_specs=[ANY] * 7,
        out_specs=(ANY, ANY, ANY, VM, VM),
        scratch_shapes=[
            pltpu.VMEM((8, 128), i32),
            pltpu.VMEM(citations.shape, i32),
            pltpu.VMEM(queries.shape, bf),
            pltpu.VMEM(suffix_keys.shape, bf),
            pltpu.VMEM(suffix_values.shape, bf),
            pltpu.VMEM(fresh_keys.shape, bf),
            pltpu.VMEM(fresh_values.shape, bf),
            dma((6,)),
            dma((3,)),
            dma((3, chips)),
            dma((3, chips)),
            dma((3, chips)),
            dma((3, chips)),
        ],
        compiler_params=pltpu.CompilerParams(
            collective_id=0, has_side_effects=True, vmem_limit_bytes=LIMIT
        ),
        name="gather_queries",
    )(queries, suffix_keys, suffix_values, fresh_keys, fresh_values, citations, selected)

    out_all, stat_all = pl.pallas_call(
        slot_kernel,
        out_shape=(
            jax.ShapeDtypeStruct((n, 2, HD, rows // 2), bf),
            jax.ShapeDtypeStruct((n, 2, 8, rows // 2), f32),
        ),
        in_specs=[SM, ANY, ANY, ANY, ANY],
        out_specs=(VM, VM),
        scratch_shapes=[
            pltpu.VMEM((n, tokens, width), bf),
            pltpu.VMEM((n, cite_count, picks), i32),
            pltpu.VMEM(passage_keys.shape, bf),
            pltpu.VMEM(passage_values.shape, bf),
            pltpu.VMEM((local, HD + ONES, length), bf),
            pltpu.VMEM((n, HD + ONES, rows), f32),
            pltpu.VMEM((n, 8, rows), f32),
            pltpu.VMEM((2, 8, rows // 2), f32),
            pltpu.VMEM((length, picks), bf),
            pltpu.VMEM((length, rows // 2), f32),
            pltpu.VMEM((length, rows // 2), f32),
            pltpu.SMEM((n * cite_count + 1,), i32),
            dma((4,)),
        ],
        compiler_params=pltpu.CompilerParams(vmem_limit_bytes=LIMIT),
        name="passage_slots",
    )(cite_all, q_all, sel_all, passage_keys, passage_values)

    return pl.pallas_call(
        functools.partial(merge_kernel, n, kv),
        out_shape=jax.ShapeDtypeStruct((1, tokens // kv, width * kv), bf),
        in_specs=[ANY] * 4,
        out_specs=VM,
        scratch_shapes=[
            pltpu.VMEM((HD + ONES, rows), f32),
            pltpu.VMEM((8, rows), f32),
            *(
                [
                    pltpu.VMEM((chips, 2, HD, rows // 2), bf),
                    pltpu.VMEM((chips, 2, 8, rows // 2), f32),
                ]
                * 4
            ),
            pltpu.VMEM((2, kv, tokens // kv, width // 2), bf),
            pltpu.VMEM((2, kv, tokens // kv, width // 2), bf),
            dma((2,)),
            *([dma((2, 2, chips))] * 5),
            dma((2, kv)),
            dma((2, kv)),
        ],
        compiler_params=pltpu.CompilerParams(
            collective_id=1, has_side_effects=True, vmem_limit_bytes=MERGE_LIMIT
        ),
        name="merge_groups",
    )(out_all, stat_all, host_acc, host_max)


def solution(mesh):
    placed = (
        P("pass", None, "kv"),
        P("pass", None, "kv"),
        P("pass", None, "kv"),
        P("pass", None, "kv"),
        P("pass", None, "kv"),
        P("pass", None, None, "kv"),
        P("pass", None, None, "kv"),
        P("pass", None),
        P("pass", None, None),
    )
    return jax.shard_map(
        functools.partial(body, mesh.shape["pass"], mesh.shape["kv"]),
        mesh=mesh,
        in_specs=placed,
        out_specs=P("pass", "kv", None),
        check_vma=False,
    )
```

```python
import functools
import math

import jax
import jax.numpy as jnp
from jax import lax
from jax.experimental import pallas as pl
from jax.experimental.pallas import tpu as pltpu
from jax.sharding import PartitionSpec as P

HD = 128
MESH = pl.DeviceIdType.MESH
very_low = -1e30
FACTOR = math.log2(math.e) / math.sqrt(HD)
ONES = 16
PMOST = 4
HALVES = 2
CHUNK = 256
KEYS = 256


def nt_dot(a, b):
    return lax.dot_general(a, b, (((1,), (1,)), ((), ())), preferred_element_type=jnp.float32)


def nn_dot(a, b):
    return jnp.dot(a, b, preferred_element_type=jnp.float32)


def stack_heads(rows, group_size):
    return jnp.concatenate([rows[:, g * HD : (g + 1) * HD] for g in range(group_size)], axis=0)


def fused_kernel(
    n,
    kv,
    q_ref,
    sk_ref,
    sv_ref,
    fk_ref,
    fv_ref,
    k_hbm,
    v_hbm,
    cite_ref,
    sel_ref,
    result,
    cite_buf,
    cite_in,
    sk_buf,
    sv_buf,
    fk_buf,
    fv_buf,
    k_ref,
    v_ref,
    v_t,
    q_low,
    q_high,
    cite_all,
    sel_all,
    bias,
    first,
    second,
    peak,
    slot_acc,
    slot_top,
    host_acc,
    host_max,
    mine_acc,
    mine_stat,
    away_out,
    away_stat,
    pair_out,
    pair_stat,
    send_out,
    send_stat,
    got_out,
    got_stat,
    kv_send,
    kv_recv,
    cites,
    slot_request,
    slot_cite,
    pair_slot,
    pair_live,
    in_sem,
    own_sem,
    gather_send,
    gather_recv,
    near_send,
    near_recv,
    pair_send_sem,
    pair_recv_sem,
    send_sem,
    recv_sem,
    kv_send_sem,
    kv_recv_sem,
):
    q_all = (q_low, q_high)
    me = lax.axis_index("pass")
    my_kv = lax.axis_index("kv")
    chip, core = me // 2, me % 2
    chips = n // 2
    sibling = chip * 2 + (1 - core)
    tokens = q_ref.shape[1]
    group_size = q_ref.shape[2] // HD
    heads = group_size // HALVES
    lanes = heads * tokens
    cut = heads * HD
    part = tokens // kv
    local, length, _ = k_ref.shape
    cite_count, picks = sel_all.shape[1:]
    slots = local * PMOST

    def target_chip(off):
        return (chip + off) % chips

    def origin(off, lane):
        return ((chip + chips - off) % chips) * 2 + lane

    loads = [
        pltpu.make_async_copy(source, place, in_sem.at[i])
        for i, (source, place) in enumerate(
            (
                (cite_ref, cite_in),
                (v_hbm, v_ref),
                (fk_ref, fk_buf),
                (fv_ref, fv_buf),
                (sk_ref, sk_buf),
                (sv_ref, sv_buf),
                (k_hbm, k_ref),
            )
        )
    ]
    for copy in loads:
        copy.start()

    sources = [cite_buf, sel_ref.at[0]] + [
        q_ref.at[0, :, h * cut : (h + 1) * cut] for h in range(HALVES)
    ]

    def place_of(i, slot):
        if i == 0:
            return cite_all.at[slot]
        if i == 1:
            return sel_all.at[slot]
        return q_all[i - 2].at[slot]

    own = [pltpu.make_async_copy(sources[i], place_of(i, me), own_sem.at[i]) for i in range(4)]
    for i in (2, 3, 1):
        own[i].start()
    barrier = pltpu.get_barrier_semaphore()
    for other in [sibling] + [target_chip(off) * 2 + core for off in range(1, chips)]:
        pl.semaphore_signal(barrier, inc=1, device_id={"pass": other}, device_id_type=MESH)
    for off in range(1, kv):
        pl.semaphore_signal(
            barrier, inc=1, device_id={"kv": (my_kv + off) % kv}, device_id_type=MESH
        )
    cite_buf[...] = jnp.zeros_like(cite_buf)
    loads[0].wait()
    cite_buf[0:1, 0:cite_count] = cite_in[...]
    own[0].start()
    pl.semaphore_wait(barrier, chips + kv - 1)

    def far(i, off, slot):
        return pltpu.make_async_remote_copy(
            src_ref=sources[i],
            dst_ref=place_of(i, slot),
            send_sem=gather_send.at[i, off],
            recv_sem=gather_recv.at[i, off],
            device_id={"pass": target_chip(off) * 2 + core},
            device_id_type=MESH,
        )

    def near(i, off, slot):
        return pltpu.make_async_remote_copy(
            src_ref=sources[i] if off == 0 else place_of(i, slot),
            dst_ref=place_of(i, slot),
            send_sem=near_send.at[i, off],
            recv_sem=near_recv.at[i, off],
            device_id={"pass": sibling},
            device_id_type=MESH,
        )

    sends = []

    def launch(copy):
        copy.start()
        sends.append(copy)

    for i in range(4):
        for off in range(1, chips):
            launch(far(i, off, me))
        launch(near(i, 0, me))

    def pass_on(i):
        for off in range(1, chips):
            slot = origin(off, core)
            far(i, off, slot).wait_recv()
            launch(near(i, off, slot))

    def settle(i):
        for off in range(chips):
            near(i, off, origin(off, 1 - core)).wait_recv()

    loads[1].wait()
    for p in range(local):
        v_t[p, 0:HD, :] = v_ref[p].T
        v_t[p, HD:, :] = jnp.ones((ONES, length), jnp.bfloat16)
    pass_on(0)
    pass_on(1)

    for copy in loads[2:]:
        copy.wait()
    for copy in own:
        copy.wait()
    fresh = fk_ref.shape[1] * fk_ref.shape[2]
    fk = fk_buf[0].reshape(fresh, HD)
    fv_t = fv_buf[0].reshape(fresh, HD).T
    fv_t = jnp.concatenate([fv_t, jnp.ones((ONES, fresh), jnp.bfloat16)], axis=0)
    sv_t = sv_buf[0].astype(jnp.float32).T.astype(jnp.bfloat16)
    sv_t = jnp.concatenate([sv_t, jnp.ones((ONES, tokens), jnp.bfloat16)], axis=0)
    for h in range(HALVES):
        block = stack_heads(q_all[h][me], heads)
        fs = nt_dot(fk, block)
        ss = nt_dot(sk_buf[0], block)
        key_at = lax.broadcasted_iota(jnp.int32, (tokens, lanes), 0)
        token_at = lax.broadcasted_iota(jnp.int32, (tokens, lanes), 1) % tokens
        ss = jnp.where(key_at <= token_at, ss, very_low)
        top = jnp.maximum(
            jnp.max(fs, axis=0, keepdims=True), jnp.max(ss, axis=0, keepdims=True)
        )
        fw = jnp.exp2((fs - top) * FACTOR).astype(jnp.bfloat16)
        sw = jnp.exp2((ss - top) * FACTOR).astype(jnp.bfloat16)
        host_acc[h] = nn_dot(fv_t, fw) + nn_dot(sv_t, sw)
        host_max[h] = jnp.broadcast_to(top, (8, lanes))

    settle(0)
    settle(1)
    to_scalar = pltpu.make_async_copy(cite_all, cites, in_sem.at[0])
    to_scalar.start()
    pass_on(2)
    to_scalar.wait()
    for i in range(slots):
        slot_request[i] = 0
        slot_cite[i] = 0

    def tabulate(r, counts):
        names = [cites[r, 0, c] for c in range(cite_count)]
        after = []
        for p in range(local):
            name = me * local + p
            hit, at = jnp.int32(0), jnp.int32(0)
            for c in range(cite_count):
                same = (names[c] == name).astype(jnp.int32)
                hit = jnp.maximum(hit, same)
                at = jnp.maximum(at, same * c)
            rank = counts[p]
            pair_live[r * local + p] = hit
            pair_slot[r * local + p] = p * PMOST + jnp.minimum(rank, PMOST - 1)
            for k in range(PMOST):
                here = hit * (rank == k).astype(jnp.int32)
                i = p * PMOST + k
                slot_request[i] = slot_request[i] + here * r
                slot_cite[i] = slot_cite[i] + here * at
            after.append(rank + hit)
        return tuple(after)

    lax.fori_loop(0, n, tabulate, (jnp.int32(0),) * local)

    def fill_bias(i, carry):
        at = lax.broadcasted_iota(jnp.int32, (length, picks), 0)
        picked = sel_all[slot_request[i], pl.ds(slot_cite[i], 1), :]
        bias[i] = jnp.where(at == picked, very_low, 0.0).astype(jnp.bfloat16)
        return carry

    lax.fori_loop(0, slots, fill_bias, 0)
    settle(2)

    steps = [slice(lo, lo + KEYS) for lo in range(0, length, KEYS)]

    def score_steps(h, i, place, side):
        p = i // PMOST
        q = stack_heads(q_all[h][slot_request[i]], heads)
        q = jnp.concatenate([q, jnp.ones((lanes, picks), jnp.bfloat16)], axis=1)
        highest = None
        for at in steps:
            keys = jnp.concatenate([k_ref[p, at, :], bias[i, at, :]], axis=1)
            s = nt_dot(keys, q)
            place[at, :] = s
            here = jnp.max(s.reshape(KEYS // 8, 8, lanes), axis=0)
            highest = here if highest is None else jnp.maximum(highest, here)
            yield
        peak[side] = jnp.broadcast_to(jnp.max(highest, axis=0, keepdims=True), (8, lanes))

    def weigh_steps(i, place, side):
        p = i // PMOST
        top = peak[side]
        slot_top[i] = top
        added = None
        for at in steps:
            w = jnp.exp2((place[at, :] - top[0:1]) * FACTOR).astype(jnp.bfloat16)
            here = nn_dot(v_t[p, :, at], w)
            added = here if added is None else added + here
            yield
        slot_acc[i] = added

    def together(*parts):
        waiting = list(parts)
        while waiting:
            waiting = [part for part in waiting if next(part, True) is None]

    def two_slots(h):
        def step(t, carry):
            i = 2 * t
            together(weigh_steps(i, first, 0), score_steps(h, i + 1, second, 1))
            later = jnp.minimum(i + 2, slots - 1)
            together(weigh_steps(i + 1, second, 1), score_steps(h, later, first, 0))
            return carry

        return step

    def flash_merge(outs, stats):
        ceiling = stats[0][0]
        for top, _ in stats[1:]:
            ceiling = jnp.maximum(ceiling, top)
        numer, denom = 0.0, 0.0
        for out, (top, weight) in zip(outs, stats):
            scale = jnp.exp2((top - ceiling) * FACTOR)
            if out.dtype == jnp.bfloat16:
                scale = weight * scale
                numer = numer + out.astype(jnp.float32) * scale
                denom = denom + scale
            else:
                numer = numer + out * scale
                denom = denom + weight * scale
        return ceiling, numer, denom

    def of_request(r):
        outs, stats = [], []
        for p in range(local):
            i, live = pair_slot[r * local + p], pair_live[r * local + p].astype(jnp.float32)
            block = slot_acc[i]
            top = slot_top[i][0:1] * live + very_low * (1.0 - live)
            outs.append(block[0:HD] * live)
            stats.append((top, block[HD : HD + 1] * live))
        return flash_merge(outs, stats)

    def stat_block(top, denom):
        return jnp.concatenate(
            [jnp.broadcast_to(top, (4, lanes)), jnp.broadcast_to(denom, (4, lanes))]
        )

    def stats_of(block):
        return block[0:1, :], block[4:5, :]

    def to_sibling(i, h, off):
        source, place = ((away_out, pair_out), (away_stat, pair_stat))[i]
        return pltpu.make_async_remote_copy(
            src_ref=source.at[off, h],
            dst_ref=place.at[off, h],
            send_sem=pair_send_sem.at[i, h, off],
            recv_sem=pair_recv_sem.at[i, h, off],
            device_id={"pass": sibling},
            device_id_type=MESH,
        )

    def to_chip(i, h, off):
        source, place = ((send_out, got_out), (send_stat, got_stat))[i]
        return pltpu.make_async_remote_copy(
            src_ref=source.at[off, h],
            dst_ref=place.at[off, h],
            send_sem=send_sem.at[i, h, off],
            recv_sem=recv_sem.at[i, h, off],
            device_id={"pass": target_chip(off) * 2 + core},
            device_id_type=MESH,
        )

    def across(h, off, target, slot):
        return pltpu.make_async_remote_copy(
            src_ref=kv_send.at[h, target],
            dst_ref=kv_recv.at[h, slot],
            send_sem=kv_send_sem.at[h, off],
            recv_sem=kv_recv_sem.at[h, off],
            device_id={"kv": target},
            device_id_type=MESH,
        )

    order = list(range(1, chips)) + [0]

    def collect(h):
        for off in order:
            top, numer, denom = of_request(target_chip(off) * 2 + 1 - core)
            away_out[off, h] = (numer * (1.0 / jnp.maximum(denom, 1.0))).astype(jnp.bfloat16)
            away_stat[off, h] = stat_block(top, denom)
            for i in (1, 0):
                launch(to_sibling(i, h, off))
        for off in order:
            top, numer, denom = of_request(target_chip(off) * 2 + core)
            mine_acc[off, h] = numer
            mine_stat[off, h] = stat_block(top, denom)

    def of_chip(h, off):
        for i in range(2):
            to_sibling(i, h, off).wait_recv()
        return (
            [mine_acc[off, h], pair_out[off, h]],
            [stats_of(mine_stat[off, h]), stats_of(pair_stat[off, h])],
        )

    def exchange(h):
        for off in range(1, chips):
            top, numer, denom = flash_merge(*of_chip(h, off))
            send_out[off, h] = (numer * (1.0 / jnp.maximum(denom, 1.0))).astype(jnp.bfloat16)
            send_stat[off, h] = stat_block(top, denom)
            for i in (1, 0):
                launch(to_chip(i, h, off))

    def finish(h):
        outs, stats = of_chip(h, 0)
        outs.append(host_acc[h, 0:HD])
        stats.append((host_max[h, 0:1], host_acc[h, HD : HD + 1]))
        for off in range(1, chips):
            for i in range(2):
                to_chip(i, h, off).wait_recv()
            outs.append(got_out[off, h])
            stats.append(stats_of(got_stat[off, h]))
        _, numer, denom = flash_merge(outs, stats)
        done = (numer / denom).T
        for j in range(kv):
            block = [done[g * tokens + j * part : g * tokens + (j + 1) * part] for g in range(heads)]
            kv_send[h, j] = jnp.concatenate(block, axis=1).astype(jnp.bfloat16)
        for off in range(1, kv):
            launch(across(h, off, (my_kv + off) % kv, my_kv))
        kv_recv[h, my_kv] = kv_send[h, my_kv]

    pairs, early = slots // 2, slots // 8
    together(score_steps(0, 0, first, 0))
    lax.fori_loop(0, early, two_slots(0), 0)
    pass_on(3)
    lax.fori_loop(early, pairs, two_slots(0), 0)
    collect(0)
    settle(3)
    together(score_steps(1, 0, first, 0))
    lax.fori_loop(0, early, two_slots(1), 0)
    exchange(0)
    lax.fori_loop(early, pairs, two_slots(1), 0)
    collect(1)
    exchange(1)
    finish(0)
    finish(1)
    for h in range(HALVES):
        for off in range(1, kv):
            across(h, off, (my_kv + off) % kv, (my_kv + kv - off) % kv).wait_recv()
        for i in range(kv):
            lo = (i * HALVES + h) * cut
            result[0, :, lo : lo + cut] = kv_recv[h, i]
    for copy in sends:
        copy.wait_send()


VM = pl.BlockSpec(memory_space=pltpu.VMEM)
ANY = pl.BlockSpec(memory_space=pl.ANY)
LIMIT = 62 * 1024 * 1024


def body(
    n,
    kv,
    queries,
    suffix_keys,
    suffix_values,
    passage_keys,
    passage_values,
    fresh_keys,
    fresh_values,
    citations,
    selected,
):
    _, tokens, width = queries.shape
    lanes = tokens * width // HD // HALVES
    local, length, _ = passage_keys.shape
    _, cite_count, picks = selected.shape
    chips = n // 2
    slots = local * PMOST
    bf, f32, i32 = jnp.bfloat16, jnp.float32, jnp.int32
    dma = pltpu.SemaphoreType.DMA
    tall = HD + ONES
    out_block = pltpu.VMEM((chips, HALVES, HD, lanes), bf)
    stat_block = pltpu.VMEM((chips, HALVES, 8, lanes), f32)
    kv_block = pltpu.VMEM((HALVES, kv, tokens // kv, width // HALVES), bf)
    return pl.pallas_call(
        functools.partial(fused_kernel, n, kv),
        out_shape=jax.ShapeDtypeStruct((1, tokens // kv, width * kv), bf),
        in_specs=[ANY] * 9,
        out_specs=VM,
        scratch_shapes=[
            pltpu.VMEM((8, 128), i32),
            pltpu.VMEM(citations.shape, i32),
            pltpu.VMEM(suffix_keys.shape, bf),
            pltpu.VMEM(suffix_values.shape, bf),
            pltpu.VMEM(fresh_keys.shape, bf),
            pltpu.VMEM(fresh_values.shape, bf),
            pltpu.VMEM(passage_keys.shape, bf),
            pltpu.VMEM(passage_values.shape, bf),
            pltpu.VMEM((local, tall, length), bf),
            pltpu.VMEM((n, tokens, width // HALVES), bf),
            pltpu.VMEM((n, tokens, width // HALVES), bf),
            pltpu.VMEM((n, 8, 128), i32),
            pltpu.VMEM((n, cite_count, picks), i32),
            pltpu.VMEM((slots, length, picks), bf),
            pltpu.VMEM((length, lanes), f32),
            pltpu.VMEM((length, lanes), f32),
            pltpu.VMEM((2, 8, lanes), f32),
            pltpu.VMEM((slots, tall, lanes), f32),
            pltpu.VMEM((slots, 8, lanes), f32),
            pltpu.VMEM((HALVES, tall, lanes), f32),
            pltpu.VMEM((HALVES, 8, lanes), f32),
            pltpu.VMEM((chips, HALVES, HD, lanes), f32),
            stat_block,
            *([out_block, stat_block] * 4),
            kv_block,
            kv_block,
            pltpu.SMEM((n, 8, 128), i32),
            pltpu.SMEM((slots,), i32),
            pltpu.SMEM((slots,), i32),
            pltpu.SMEM((n * local,), i32),
            pltpu.SMEM((n * local,), i32),
            dma((7,)),
            dma((4,)),
            *([dma((4, chips))] * 4),
            *([dma((2, HALVES, chips))] * 4),
            dma((HALVES, kv)),
            dma((HALVES, kv)),
        ],
        compiler_params=pltpu.CompilerParams(
            collective_id=0, has_side_effects=True, vmem_limit_bytes=LIMIT
        ),
        name="fused_attention",
    )(
        queries,
        suffix_keys,
        suffix_values,
        fresh_keys,
        fresh_values,
        passage_keys,
        passage_values,
        citations,
        selected,
    )


def solution(mesh):
    placed = (
        P("pass", None, "kv"),
        P("pass", None, "kv"),
        P("pass", None, "kv"),
        P("pass", None, "kv"),
        P("pass", None, "kv"),
        P("pass", None, None, "kv"),
        P("pass", None, None, "kv"),
        P("pass", None),
        P("pass", None, None),
    )
    return jax.shard_map(
        functools.partial(body, mesh.shape["pass"], mesh.shape["kv"]),
        mesh=mesh,
        in_specs=placed,
        out_specs=P("pass", "kv", None),
        check_vma=False,
    )
```

```python
import functools
import math

import jax
import jax.numpy as jnp
from jax import lax
from jax.experimental import pallas as pl
from jax.experimental.pallas import tpu as pltpu
from jax.sharding import PartitionSpec as P

HD = 128
MESH = pl.DeviceIdType.MESH
very_low = -1e30
FACTOR = math.log2(math.e) / math.sqrt(HD)
ONES = 16
PMOST = 4
HALVES = 2
CHUNK = 256
KEYS = 256


def nt_dot(a, b):
    return lax.dot_general(a, b, (((1,), (1,)), ((), ())), preferred_element_type=jnp.float32)


def nn_dot(a, b):
    return jnp.dot(a, b, preferred_element_type=jnp.float32)


def stack_heads(rows, group_size):
    return jnp.concatenate([rows[:, g * HD : (g + 1) * HD] for g in range(group_size)], axis=0)


def fused_kernel(
    n,
    kv,
    q_ref,
    sk_ref,
    sv_ref,
    fk_ref,
    fv_ref,
    k_hbm,
    v_hbm,
    cite_ref,
    sel_ref,
    result,
    cite_buf,
    cite_in,
    sk_buf,
    sv_buf,
    fk_buf,
    fv_buf,
    k_ref,
    v_ref,
    v_t,
    q_low,
    q_high,
    cite_all,
    sel_all,
    bias,
    first,
    second,
    peak,
    slot_acc,
    slot_top,
    host_acc,
    host_max,
    mine_acc,
    mine_stat,
    away_out,
    away_stat,
    pair_out,
    pair_stat,
    send_out,
    send_stat,
    got_out,
    got_stat,
    kv_send,
    kv_recv,
    cites,
    slot_request,
    slot_cite,
    pair_slot,
    pair_live,
    in_sem,
    own_sem,
    gather_send,
    gather_recv,
    near_send,
    near_recv,
    pair_send_sem,
    pair_recv_sem,
    send_sem,
    recv_sem,
    kv_send_sem,
    kv_recv_sem,
):
    q_all = (q_low, q_high)
    me = lax.axis_index("pass")
    my_kv = lax.axis_index("kv")
    chip, core = me // 2, me % 2
    chips = n // 2
    sibling = chip * 2 + (1 - core)
    tokens = q_ref.shape[1]
    group_size = q_ref.shape[2] // HD
    heads = group_size // HALVES
    lanes = heads * tokens
    cut = heads * HD
    part = tokens // kv
    local, length, _ = k_ref.shape
    cite_count, picks = sel_all.shape[1:]
    slots = local * PMOST

    def target_chip(off):
        return (chip + off) % chips

    def origin(off, lane):
        return ((chip + chips - off) % chips) * 2 + lane

    loads = [
        pltpu.make_async_copy(source, place, in_sem.at[i])
        for i, (source, place) in enumerate(
            (
                (cite_ref, cite_in),
                (v_hbm, v_ref),
                (fk_ref, fk_buf),
                (fv_ref, fv_buf),
                (sk_ref, sk_buf),
                (sv_ref, sv_buf),
                (k_hbm, k_ref),
            )
        )
    ]
    for copy in loads:
        copy.start()

    sources = [cite_buf, sel_ref.at[0]] + [
        q_ref.at[0, :, h * cut : (h + 1) * cut] for h in range(HALVES)
    ]

    def place_of(i, slot):
        if i == 0:
            return cite_all.at[slot]
        if i == 1:
            return sel_all.at[slot]
        return q_all[i - 2].at[slot]

    own = [pltpu.make_async_copy(sources[i], place_of(i, me), own_sem.at[i]) for i in range(4)]
    for i in (2, 3, 1):
        own[i].start()
    barrier = pltpu.get_barrier_semaphore()
    for other in [sibling] + [target_chip(off) * 2 + core for off in range(1, chips)]:
        pl.semaphore_signal(barrier, inc=1, device_id={"pass": other}, device_id_type=MESH)
    for off in range(1, kv):
        pl.semaphore_signal(
            barrier, inc=1, device_id={"kv": (my_kv + off) % kv}, device_id_type=MESH
        )
    cite_buf[...] = jnp.zeros_like(cite_buf)
    loads[0].wait()
    cite_buf[0:1, 0:cite_count] = cite_in[...]
    own[0].start()
    pl.semaphore_wait(barrier, chips + kv - 1)

    def far(i, off, slot):
        return pltpu.make_async_remote_copy(
            src_ref=sources[i],
            dst_ref=place_of(i, slot),
            send_sem=gather_send.at[i, off],
            recv_sem=gather_recv.at[i, off],
            device_id={"pass": target_chip(off) * 2 + core},
            device_id_type=MESH,
        )

    def near(i, off, slot):
        return pltpu.make_async_remote_copy(
            src_ref=sources[i] if off == 0 else place_of(i, slot),
            dst_ref=place_of(i, slot),
            send_sem=near_send.at[i, off],
            recv_sem=near_recv.at[i, off],
            device_id={"pass": sibling},
            device_id_type=MESH,
        )

    sends = []

    def launch(copy):
        copy.start()
        sends.append(copy)

    for i in range(4):
        for off in range(1, chips):
            launch(far(i, off, me))
        launch(near(i, 0, me))

    def pass_on(i):
        for off in range(1, chips):
            slot = origin(off, core)
            far(i, off, slot).wait_recv()
            launch(near(i, off, slot))

    def settle(i):
        for off in range(chips):
            near(i, off, origin(off, 1 - core)).wait_recv()

    loads[1].wait()
    for p in range(local):
        v_t[p, 0:HD, :] = v_ref[p].T
        v_t[p, HD:, :] = jnp.ones((ONES, length), jnp.bfloat16)
    pass_on(0)
    pass_on(1)

    for copy in loads[2:]:
        copy.wait()
    for copy in own:
        copy.wait()
    settle(0)
    settle(1)
    to_scalar = pltpu.make_async_copy(cite_all, cites, in_sem.at[0])
    to_scalar.start()
    to_scalar.wait()
    for i in range(slots):
        slot_request[i] = 0
        slot_cite[i] = 0

    def tabulate(r, counts):
        names = [cites[r, 0, c] for c in range(cite_count)]
        after = []
        for p in range(local):
            name = me * local + p
            hit, at = jnp.int32(0), jnp.int32(0)
            for c in range(cite_count):
                same = (names[c] == name).astype(jnp.int32)
                hit = jnp.maximum(hit, same)
                at = jnp.maximum(at, same * c)
            rank = counts[p]
            pair_live[r * local + p] = hit
            pair_slot[r * local + p] = p * PMOST + jnp.minimum(rank, PMOST - 1)
            for k in range(PMOST):
                here = hit * (rank == k).astype(jnp.int32)
                i = p * PMOST + k
                slot_request[i] = slot_request[i] + here * r
                slot_cite[i] = slot_cite[i] + here * at
            after.append(rank + hit)
        return tuple(after)

    lax.fori_loop(0, n, tabulate, (jnp.int32(0),) * local)
    pass_on(2)

    def fill_bias(i, carry):
        at = lax.broadcasted_iota(jnp.int32, (length, picks), 0)
        picked = sel_all[slot_request[i], pl.ds(slot_cite[i], 1), :]
        bias[i] = jnp.where(at == picked, very_low, 0.0).astype(jnp.bfloat16)
        return carry

    lax.fori_loop(0, slots, fill_bias, 0)
    settle(2)

    steps = [slice(lo, lo + KEYS) for lo in range(0, length, KEYS)]

    def score_steps(h, i, place, side):
        p = i // PMOST
        q = stack_heads(q_all[h][slot_request[i]], heads)
        q = jnp.concatenate([q, jnp.ones((lanes, picks), jnp.bfloat16)], axis=1)
        highest = None
        for at in steps:
            keys = jnp.concatenate([k_ref[p, at, :], bias[i, at, :]], axis=1)
            s = nt_dot(keys, q)
            place[at, :] = s
            here = jnp.max(s.reshape(KEYS // 8, 8, lanes), axis=0)
            highest = here if highest is None else jnp.maximum(highest, here)
            yield
        peak[side] = jnp.broadcast_to(jnp.max(highest, axis=0, keepdims=True), (8, lanes))

    def weigh_steps(i, place, side):
        p = i // PMOST
        top = peak[side]
        slot_top[i] = top
        added = None
        for at in steps:
            w = jnp.exp2((place[at, :] - top[0:1]) * FACTOR).astype(jnp.bfloat16)
            here = nn_dot(v_t[p, :, at], w)
            added = here if added is None else added + here
            yield
        slot_acc[i] = added

    def together(*parts):
        waiting = list(parts)
        while waiting:
            waiting = [part for part in waiting if next(part, True) is None]

    def two_slots(h):
        def step(t, carry):
            i = 2 * t
            together(weigh_steps(i, first, 0), score_steps(h, i + 1, second, 1))
            later = jnp.minimum(i + 2, slots - 1)
            together(weigh_steps(i + 1, second, 1), score_steps(h, later, first, 0))
            return carry

        return step

    def flash_merge(outs, stats):
        ceiling = stats[0][0]
        for top, _ in stats[1:]:
            ceiling = jnp.maximum(ceiling, top)
        numer, denom = 0.0, 0.0
        for out, (top, weight) in zip(outs, stats):
            scale = jnp.exp2((top - ceiling) * FACTOR)
            if out.dtype == jnp.bfloat16:
                scale = weight * scale
                numer = numer + out.astype(jnp.float32) * scale
                denom = denom + scale
            else:
                numer = numer + out * scale
                denom = denom + weight * scale
        return ceiling, numer, denom

    def of_request(r):
        outs, stats = [], []
        for p in range(local):
            i, live = pair_slot[r * local + p], pair_live[r * local + p].astype(jnp.float32)
            block = slot_acc[i]
            top = slot_top[i][0:1] * live + very_low * (1.0 - live)
            outs.append(block[0:HD] * live)
            stats.append((top, block[HD : HD + 1] * live))
        return flash_merge(outs, stats)

    def stat_block(top, denom):
        return jnp.concatenate(
            [jnp.broadcast_to(top, (4, lanes)), jnp.broadcast_to(denom, (4, lanes))]
        )

    def stats_of(block):
        return block[0:1, :], block[4:5, :]

    def to_sibling(i, h, off):
        source, place = ((away_out, pair_out), (away_stat, pair_stat))[i]
        return pltpu.make_async_remote_copy(
            src_ref=source.at[off, h],
            dst_ref=place.at[off, h],
            send_sem=pair_send_sem.at[i, h, off],
            recv_sem=pair_recv_sem.at[i, h, off],
            device_id={"pass": sibling},
            device_id_type=MESH,
        )

    def to_chip(i, h, off):
        source, place = ((send_out, got_out), (send_stat, got_stat))[i]
        return pltpu.make_async_remote_copy(
            src_ref=source.at[off, h],
            dst_ref=place.at[off, h],
            send_sem=send_sem.at[i, h, off],
            recv_sem=recv_sem.at[i, h, off],
            device_id={"pass": target_chip(off) * 2 + core},
            device_id_type=MESH,
        )

    def across(h, off, target, slot):
        return pltpu.make_async_remote_copy(
            src_ref=kv_send.at[h, target],
            dst_ref=kv_recv.at[h, slot],
            send_sem=kv_send_sem.at[h, off],
            recv_sem=kv_recv_sem.at[h, off],
            device_id={"kv": target},
            device_id_type=MESH,
        )

    order = list(range(1, chips)) + [0]

    def collect(h):
        for off in order:
            top, numer, denom = of_request(target_chip(off) * 2 + 1 - core)
            away_out[off, h] = (numer * (1.0 / jnp.maximum(denom, 1.0))).astype(jnp.bfloat16)
            away_stat[off, h] = stat_block(top, denom)
            for i in (1, 0):
                launch(to_sibling(i, h, off))
        for off in order:
            top, numer, denom = of_request(target_chip(off) * 2 + core)
            mine_acc[off, h] = numer
            mine_stat[off, h] = stat_block(top, denom)

    def of_chip(h, off):
        for i in range(2):
            to_sibling(i, h, off).wait_recv()
        return (
            [mine_acc[off, h], pair_out[off, h]],
            [stats_of(mine_stat[off, h]), stats_of(pair_stat[off, h])],
        )

    def exchange(h):
        for off in range(1, chips):
            top, numer, denom = flash_merge(*of_chip(h, off))
            send_out[off, h] = (numer * (1.0 / jnp.maximum(denom, 1.0))).astype(jnp.bfloat16)
            send_stat[off, h] = stat_block(top, denom)
            for i in (1, 0):
                launch(to_chip(i, h, off))

    def finish(h):
        outs, stats = of_chip(h, 0)
        outs.append(host_acc[h, 0:HD])
        stats.append((host_max[h, 0:1], host_acc[h, HD : HD + 1]))
        for off in range(1, chips):
            for i in range(2):
                to_chip(i, h, off).wait_recv()
            outs.append(got_out[off, h])
            stats.append(stats_of(got_stat[off, h]))
        _, numer, denom = flash_merge(outs, stats)
        done = (numer / denom).T
        for j in range(kv):
            block = [done[g * tokens + j * part : g * tokens + (j + 1) * part] for g in range(heads)]
            kv_send[h, j] = jnp.concatenate(block, axis=1).astype(jnp.bfloat16)
        for off in range(1, kv):
            launch(across(h, off, (my_kv + off) % kv, my_kv))
        kv_recv[h, my_kv] = kv_send[h, my_kv]

    def attend_host(h):
        block = stack_heads(q_all[h][me], heads)
        fs = nt_dot(fk, block)
        ss = nt_dot(sk_buf[0], block)
        key_at = lax.broadcasted_iota(jnp.int32, (tokens, lanes), 0)
        token_at = lax.broadcasted_iota(jnp.int32, (tokens, lanes), 1) % tokens
        ss = jnp.where(key_at <= token_at, ss, very_low)
        top = jnp.maximum(
            jnp.max(fs, axis=0, keepdims=True), jnp.max(ss, axis=0, keepdims=True)
        )
        fw = jnp.exp2((fs - top) * FACTOR).astype(jnp.bfloat16)
        sw = jnp.exp2((ss - top) * FACTOR).astype(jnp.bfloat16)
        host_acc[h] = nn_dot(fv_t, fw) + nn_dot(sv_t, sw)
        host_max[h] = jnp.broadcast_to(top, (8, lanes))

    pairs, early = slots // 2, slots // 8
    together(score_steps(0, 0, first, 0))
    lax.fori_loop(0, early, two_slots(0), 0)
    pass_on(3)
    lax.fori_loop(early, pairs, two_slots(0), 0)
    collect(0)
    settle(3)
    together(score_steps(1, 0, first, 0))
    lax.fori_loop(0, early, two_slots(1), 0)
    exchange(0)
    lax.fori_loop(early, pairs, two_slots(1), 0)
    collect(1)
    exchange(1)
    fresh = fk_ref.shape[1] * fk_ref.shape[2]
    fk = fk_buf[0].reshape(fresh, HD)
    fv_t = fv_buf[0].reshape(fresh, HD).T
    fv_t = jnp.concatenate([fv_t, jnp.ones((ONES, fresh), jnp.bfloat16)], axis=0)
    sv_t = sv_buf[0].astype(jnp.float32).T.astype(jnp.bfloat16)
    sv_t = jnp.concatenate([sv_t, jnp.ones((ONES, tokens), jnp.bfloat16)], axis=0)
    for h in range(HALVES):
        attend_host(h)
        finish(h)
    for h in range(HALVES):
        for off in range(1, kv):
            across(h, off, (my_kv + off) % kv, (my_kv + kv - off) % kv).wait_recv()
        for i in range(kv):
            lo = (i * HALVES + h) * cut
            result[0, :, lo : lo + cut] = kv_recv[h, i]
    for copy in sends:
        copy.wait_send()


VM = pl.BlockSpec(memory_space=pltpu.VMEM)
ANY = pl.BlockSpec(memory_space=pl.ANY)
LIMIT = 62 * 1024 * 1024


def body(
    n,
    kv,
    queries,
    suffix_keys,
    suffix_values,
    passage_keys,
    passage_values,
    fresh_keys,
    fresh_values,
    citations,
    selected,
):
    _, tokens, width = queries.shape
    lanes = tokens * width // HD // HALVES
    local, length, _ = passage_keys.shape
    _, cite_count, picks = selected.shape
    chips = n // 2
    slots = local * PMOST
    bf, f32, i32 = jnp.bfloat16, jnp.float32, jnp.int32
    dma = pltpu.SemaphoreType.DMA
    tall = HD + ONES
    out_block = pltpu.VMEM((chips, HALVES, HD, lanes), bf)
    stat_block = pltpu.VMEM((chips, HALVES, 8, lanes), f32)
    kv_block = pltpu.VMEM((HALVES, kv, tokens // kv, width // HALVES), bf)
    return pl.pallas_call(
        functools.partial(fused_kernel, n, kv),
        out_shape=jax.ShapeDtypeStruct((1, tokens // kv, width * kv), bf),
        in_specs=[ANY] * 9,
        out_specs=VM,
        scratch_shapes=[
            pltpu.VMEM((8, 128), i32),
            pltpu.VMEM(citations.shape, i32),
            pltpu.VMEM(suffix_keys.shape, bf),
            pltpu.VMEM(suffix_values.shape, bf),
            pltpu.VMEM(fresh_keys.shape, bf),
            pltpu.VMEM(fresh_values.shape, bf),
            pltpu.VMEM(passage_keys.shape, bf),
            pltpu.VMEM(passage_values.shape, bf),
            pltpu.VMEM((local, tall, length), bf),
            pltpu.VMEM((n, tokens, width // HALVES), bf),
            pltpu.VMEM((n, tokens, width // HALVES), bf),
            pltpu.VMEM((n, 8, 128), i32),
            pltpu.VMEM((n, cite_count, picks), i32),
            pltpu.VMEM((slots, length, picks), bf),
            pltpu.VMEM((length, lanes), f32),
            pltpu.VMEM((length, lanes), f32),
            pltpu.VMEM((2, 8, lanes), f32),
            pltpu.VMEM((slots, tall, lanes), f32),
            pltpu.VMEM((slots, 8, lanes), f32),
            pltpu.VMEM((HALVES, tall, lanes), f32),
            pltpu.VMEM((HALVES, 8, lanes), f32),
            pltpu.VMEM((chips, HALVES, HD, lanes), f32),
            stat_block,
            *([out_block, stat_block] * 4),
            kv_block,
            kv_block,
            pltpu.SMEM((n, 8, 128), i32),
            pltpu.SMEM((slots,), i32),
            pltpu.SMEM((slots,), i32),
            pltpu.SMEM((n * local,), i32),
            pltpu.SMEM((n * local,), i32),
            dma((7,)),
            dma((4,)),
            *([dma((4, chips))] * 4),
            *([dma((2, HALVES, chips))] * 4),
            dma((HALVES, kv)),
            dma((HALVES, kv)),
        ],
        compiler_params=pltpu.CompilerParams(
            collective_id=0, has_side_effects=True, vmem_limit_bytes=LIMIT
        ),
        name="fused_attention",
    )(
        queries,
        suffix_keys,
        suffix_values,
        fresh_keys,
        fresh_values,
        passage_keys,
        passage_values,
        citations,
        selected,
    )


def solution(mesh):
    placed = (
        P("pass", None, "kv"),
        P("pass", None, "kv"),
        P("pass", None, "kv"),
        P("pass", None, "kv"),
        P("pass", None, "kv"),
        P("pass", None, None, "kv"),
        P("pass", None, None, "kv"),
        P("pass", None),
        P("pass", None, None),
    )
    return jax.shard_map(
        functools.partial(body, mesh.shape["pass"], mesh.shape["kv"]),
        mesh=mesh,
        in_specs=placed,
        out_specs=P("pass", "kv", None),
        check_vma=False,
    )
```

```python
import functools
import math

import jax
import jax.numpy as jnp
from jax import lax
from jax.experimental import pallas as pl
from jax.experimental.pallas import tpu as pltpu
from jax.sharding import PartitionSpec as P

HD = 128
MESH = pl.DeviceIdType.MESH
very_low = -1e30
FACTOR = math.log2(math.e) / math.sqrt(HD)
ONES = 16
PMOST = 4
HALVES = 2
CHUNK = 256
KEYS = 512


def nt_dot(a, b):
    return lax.dot_general(a, b, (((1,), (1,)), ((), ())), preferred_element_type=jnp.float32)


def nn_dot(a, b):
    return jnp.dot(a, b, preferred_element_type=jnp.float32)


def stack_heads(rows, group_size):
    return jnp.concatenate([rows[:, g * HD : (g + 1) * HD] for g in range(group_size)], axis=0)


def fused_kernel(
    n,
    kv,
    q_ref,
    sk_ref,
    sv_ref,
    fk_ref,
    fv_ref,
    k_hbm,
    v_hbm,
    cite_ref,
    sel_ref,
    result,
    cite_buf,
    cite_in,
    sk_buf,
    sv_buf,
    fk_buf,
    fv_buf,
    k_ref,
    v_ref,
    v_t,
    q_low,
    q_high,
    cite_all,
    sel_all,
    bias,
    first,
    second,
    peak,
    slot_acc,
    slot_top,
    host_acc,
    host_max,
    mine_acc,
    mine_stat,
    away_out,
    away_stat,
    pair_out,
    pair_stat,
    send_out,
    send_stat,
    got_out,
    got_stat,
    kv_send,
    kv_recv,
    cites,
    slot_request,
    slot_cite,
    pair_slot,
    pair_live,
    in_sem,
    own_sem,
    gather_send,
    gather_recv,
    near_send,
    near_recv,
    pair_send_sem,
    pair_recv_sem,
    send_sem,
    recv_sem,
    kv_send_sem,
    kv_recv_sem,
):
    q_all = (q_low, q_high)
    me = lax.axis_index("pass")
    my_kv = lax.axis_index("kv")
    chip, core = me // 2, me % 2
    chips = n // 2
    sibling = chip * 2 + (1 - core)
    tokens = q_ref.shape[1]
    group_size = q_ref.shape[2] // HD
    heads = group_size // HALVES
    lanes = heads * tokens
    cut = heads * HD
    part = tokens // kv
    local, length, _ = k_ref.shape
    cite_count, picks = sel_all.shape[1:]
    slots = local * PMOST

    def target_chip(off):
        return (chip + off) % chips

    def origin(off, lane):
        return ((chip + chips - off) % chips) * 2 + lane

    loads = [
        pltpu.make_async_copy(source, place, in_sem.at[i])
        for i, (source, place) in enumerate(
            (
                (cite_ref, cite_in),
                (v_hbm, v_ref),
                (fk_ref, fk_buf),
                (fv_ref, fv_buf),
                (sk_ref, sk_buf),
                (sv_ref, sv_buf),
                (k_hbm, k_ref),
            )
        )
    ]
    for copy in loads:
        copy.start()

    sources = [cite_buf, sel_ref.at[0]] + [
        q_ref.at[0, :, h * cut : (h + 1) * cut] for h in range(HALVES)
    ]

    def place_of(i, slot):
        if i == 0:
            return cite_all.at[slot]
        if i == 1:
            return sel_all.at[slot]
        return q_all[i - 2].at[slot]

    own = [pltpu.make_async_copy(sources[i], place_of(i, me), own_sem.at[i]) for i in range(4)]
    for i in (2, 3, 1):
        own[i].start()
    barrier = pltpu.get_barrier_semaphore()
    for other in [sibling] + [target_chip(off) * 2 + core for off in range(1, chips)]:
        pl.semaphore_signal(barrier, inc=1, device_id={"pass": other}, device_id_type=MESH)
    for off in range(1, kv):
        pl.semaphore_signal(
            barrier, inc=1, device_id={"kv": (my_kv + off) % kv}, device_id_type=MESH
        )
    cite_buf[...] = jnp.zeros_like(cite_buf)
    loads[0].wait()
    cite_buf[0:1, 0:cite_count] = cite_in[...]
    own[0].start()
    pl.semaphore_wait(barrier, chips + kv - 1)

    def far(i, off, slot):
        return pltpu.make_async_remote_copy(
            src_ref=sources[i],
            dst_ref=place_of(i, slot),
            send_sem=gather_send.at[i, off],
            recv_sem=gather_recv.at[i, off],
            device_id={"pass": target_chip(off) * 2 + core},
            device_id_type=MESH,
        )

    def near(i, off, slot):
        return pltpu.make_async_remote_copy(
            src_ref=sources[i] if off == 0 else place_of(i, slot),
            dst_ref=place_of(i, slot),
            send_sem=near_send.at[i, off],
            recv_sem=near_recv.at[i, off],
            device_id={"pass": sibling},
            device_id_type=MESH,
        )

    sends = []

    def launch(copy):
        copy.start()
        sends.append(copy)

    for i in range(4):
        for off in range(1, chips):
            launch(far(i, off, me))
        launch(near(i, 0, me))

    def pass_on(i):
        for off in range(1, chips):
            slot = origin(off, core)
            far(i, off, slot).wait_recv()
            launch(near(i, off, slot))

    def settle(i):
        for off in range(chips):
            near(i, off, origin(off, 1 - core)).wait_recv()

    loads[1].wait()
    for p in range(local):
        v_t[p, 0:HD, :] = v_ref[p].T
        v_t[p, HD:, :] = jnp.ones((ONES, length), jnp.bfloat16)
    pass_on(0)
    pass_on(1)

    for copy in loads[2:]:
        copy.wait()
    for copy in own:
        copy.wait()
    settle(0)
    settle(1)
    to_scalar = pltpu.make_async_copy(cite_all, cites, in_sem.at[0])
    to_scalar.start()
    to_scalar.wait()
    for i in range(slots):
        slot_request[i] = 0
        slot_cite[i] = 0

    def tabulate(r, counts):
        names = [cites[r, 0, c] for c in range(cite_count)]
        after = []
        for p in range(local):
            name = me * local + p
            hit, at = jnp.int32(0), jnp.int32(0)
            for c in range(cite_count):
                same = (names[c] == name).astype(jnp.int32)
                hit = jnp.maximum(hit, same)
                at = jnp.maximum(at, same * c)
            rank = counts[p]
            pair_live[r * local + p] = hit
            pair_slot[r * local + p] = p * PMOST + jnp.minimum(rank, PMOST - 1)
            for k in range(PMOST):
                here = hit * (rank == k).astype(jnp.int32)
                i = p * PMOST + k
                slot_request[i] = slot_request[i] + here * r
                slot_cite[i] = slot_cite[i] + here * at
            after.append(rank + hit)
        return tuple(after)

    lax.fori_loop(0, n, tabulate, (jnp.int32(0),) * local)
    pass_on(2)

    def fill_bias(i, carry):
        at = lax.broadcasted_iota(jnp.int32, (length, picks), 0)
        picked = sel_all[slot_request[i], pl.ds(slot_cite[i], 1), :]
        bias[i] = jnp.where(at == picked, very_low, 0.0).astype(jnp.bfloat16)
        return carry

    lax.fori_loop(0, slots, fill_bias, 0)
    settle(2)

    steps = [slice(lo, lo + KEYS) for lo in range(0, length, KEYS)]

    def score_steps(h, i, place, side):
        p = i // PMOST
        q = stack_heads(q_all[h][slot_request[i]], heads)
        q = jnp.concatenate([q, jnp.ones((lanes, picks), jnp.bfloat16)], axis=1)
        highest = None
        for at in steps:
            keys = jnp.concatenate([k_ref[p, at, :], bias[i, at, :]], axis=1)
            s = nt_dot(keys, q)
            place[at, :] = s
            here = jnp.max(s.reshape(KEYS // 8, 8, lanes), axis=0)
            highest = here if highest is None else jnp.maximum(highest, here)
            yield
        peak[side] = jnp.broadcast_to(jnp.max(highest, axis=0, keepdims=True), (8, lanes))

    def weigh_steps(i, place, side):
        p = i // PMOST
        top = peak[side]
        slot_top[i] = top
        added = None
        for at in steps:
            w = jnp.exp2((place[at, :] - top[0:1]) * FACTOR).astype(jnp.bfloat16)
            here = nn_dot(v_t[p, :, at], w)
            added = here if added is None else added + here
            yield
        slot_acc[i] = added

    def together(*parts):
        waiting = list(parts)
        while waiting:
            waiting = [part for part in waiting if next(part, True) is None]

    def two_slots(h):
        def step(t, carry):
            i = 2 * t
            together(weigh_steps(i, first, 0), score_steps(h, i + 1, second, 1))
            later = jnp.minimum(i + 2, slots - 1)
            together(weigh_steps(i + 1, second, 1), score_steps(h, later, first, 0))
            return carry

        return step

    def flash_merge(outs, stats):
        ceiling = stats[0][0]
        for top, _ in stats[1:]:
            ceiling = jnp.maximum(ceiling, top)
        numer, denom = 0.0, 0.0
        for out, (top, weight) in zip(outs, stats):
            scale = jnp.exp2((top - ceiling) * FACTOR)
            if out.dtype == jnp.bfloat16:
                scale = weight * scale
                numer = numer + out.astype(jnp.float32) * scale
                denom = denom + scale
            else:
                numer = numer + out * scale
                denom = denom + weight * scale
        return ceiling, numer, denom

    def of_request(r):
        outs, stats = [], []
        for p in range(local):
            i, live = pair_slot[r * local + p], pair_live[r * local + p].astype(jnp.float32)
            block = slot_acc[i]
            top = slot_top[i][0:1] * live + very_low * (1.0 - live)
            outs.append(block[0:HD] * live)
            stats.append((top, block[HD : HD + 1] * live))
        return flash_merge(outs, stats)

    def stat_block(top, denom):
        return jnp.concatenate(
            [jnp.broadcast_to(top, (4, lanes)), jnp.broadcast_to(denom, (4, lanes))]
        )

    def stats_of(block):
        return block[0:1, :], block[4:5, :]

    def to_sibling(i, h, off):
        source, place = ((away_out, pair_out), (away_stat, pair_stat))[i]
        return pltpu.make_async_remote_copy(
            src_ref=source.at[off, h],
            dst_ref=place.at[off, h],
            send_sem=pair_send_sem.at[i, h, off],
            recv_sem=pair_recv_sem.at[i, h, off],
            device_id={"pass": sibling},
            device_id_type=MESH,
        )

    def to_chip(i, h, off):
        source, place = ((send_out, got_out), (send_stat, got_stat))[i]
        return pltpu.make_async_remote_copy(
            src_ref=source.at[off, h],
            dst_ref=place.at[off, h],
            send_sem=send_sem.at[i, h, off],
            recv_sem=recv_sem.at[i, h, off],
            device_id={"pass": target_chip(off) * 2 + core},
            device_id_type=MESH,
        )

    def across(h, off, target, slot):
        return pltpu.make_async_remote_copy(
            src_ref=kv_send.at[h, target],
            dst_ref=kv_recv.at[h, slot],
            send_sem=kv_send_sem.at[h, off],
            recv_sem=kv_recv_sem.at[h, off],
            device_id={"kv": target},
            device_id_type=MESH,
        )

    order = list(range(1, chips)) + [0]

    def collect(h):
        for off in order:
            top, numer, denom = of_request(target_chip(off) * 2 + 1 - core)
            away_out[off, h] = (numer * (1.0 / jnp.maximum(denom, 1.0))).astype(jnp.bfloat16)
            away_stat[off, h] = stat_block(top, denom)
            for i in (1, 0):
                launch(to_sibling(i, h, off))
        for off in order:
            top, numer, denom = of_request(target_chip(off) * 2 + core)
            mine_acc[off, h] = numer
            mine_stat[off, h] = stat_block(top, denom)

    def of_chip(h, off):
        for i in range(2):
            to_sibling(i, h, off).wait_recv()
        return (
            [mine_acc[off, h], pair_out[off, h]],
            [stats_of(mine_stat[off, h]), stats_of(pair_stat[off, h])],
        )

    def exchange(h):
        for off in range(1, chips):
            top, numer, denom = flash_merge(*of_chip(h, off))
            send_out[off, h] = (numer * (1.0 / jnp.maximum(denom, 1.0))).astype(jnp.bfloat16)
            send_stat[off, h] = stat_block(top, denom)
            for i in (1, 0):
                launch(to_chip(i, h, off))

    def finish(h):
        outs, stats = of_chip(h, 0)
        outs.append(host_acc[h, 0:HD])
        stats.append((host_max[h, 0:1], host_acc[h, HD : HD + 1]))
        for off in range(1, chips):
            for i in range(2):
                to_chip(i, h, off).wait_recv()
            outs.append(got_out[off, h])
            stats.append(stats_of(got_stat[off, h]))
        _, numer, denom = flash_merge(outs, stats)
        done = (numer / denom).T
        for j in range(kv):
            block = [done[g * tokens + j * part : g * tokens + (j + 1) * part] for g in range(heads)]
            kv_send[h, j] = jnp.concatenate(block, axis=1).astype(jnp.bfloat16)
        for off in range(1, kv):
            launch(across(h, off, (my_kv + off) % kv, my_kv))
        kv_recv[h, my_kv] = kv_send[h, my_kv]

    def attend_host(h):
        block = stack_heads(q_all[h][me], heads)
        fs = nt_dot(fk, block)
        ss = nt_dot(sk_buf[0], block)
        key_at = lax.broadcasted_iota(jnp.int32, (tokens, lanes), 0)
        token_at = lax.broadcasted_iota(jnp.int32, (tokens, lanes), 1) % tokens
        ss = jnp.where(key_at <= token_at, ss, very_low)
        top = jnp.maximum(
            jnp.max(fs, axis=0, keepdims=True), jnp.max(ss, axis=0, keepdims=True)
        )
        fw = jnp.exp2((fs - top) * FACTOR).astype(jnp.bfloat16)
        sw = jnp.exp2((ss - top) * FACTOR).astype(jnp.bfloat16)
        host_acc[h] = nn_dot(fv_t, fw) + nn_dot(sv_t, sw)
        host_max[h] = jnp.broadcast_to(top, (8, lanes))

    pairs, early = slots // 2, slots // 8
    together(score_steps(0, 0, first, 0))
    lax.fori_loop(0, early, two_slots(0), 0)
    pass_on(3)
    lax.fori_loop(early, pairs, two_slots(0), 0)
    collect(0)
    settle(3)
    together(score_steps(1, 0, first, 0))
    lax.fori_loop(0, early, two_slots(1), 0)
    exchange(0)
    lax.fori_loop(early, pairs, two_slots(1), 0)
    collect(1)
    exchange(1)
    fresh = fk_ref.shape[1] * fk_ref.shape[2]
    fk = fk_buf[0].reshape(fresh, HD)
    fv_t = fv_buf[0].reshape(fresh, HD).T
    fv_t = jnp.concatenate([fv_t, jnp.ones((ONES, fresh), jnp.bfloat16)], axis=0)
    sv_t = sv_buf[0].astype(jnp.float32).T.astype(jnp.bfloat16)
    sv_t = jnp.concatenate([sv_t, jnp.ones((ONES, tokens), jnp.bfloat16)], axis=0)
    for h in range(HALVES):
        attend_host(h)
        finish(h)
    for h in range(HALVES):
        for off in range(1, kv):
            across(h, off, (my_kv + off) % kv, (my_kv + kv - off) % kv).wait_recv()
        for i in range(kv):
            lo = (i * HALVES + h) * cut
            result[0, :, lo : lo + cut] = kv_recv[h, i]
    for copy in sends:
        copy.wait_send()


VM = pl.BlockSpec(memory_space=pltpu.VMEM)
ANY = pl.BlockSpec(memory_space=pl.ANY)
LIMIT = 62 * 1024 * 1024


def body(
    n,
    kv,
    queries,
    suffix_keys,
    suffix_values,
    passage_keys,
    passage_values,
    fresh_keys,
    fresh_values,
    citations,
    selected,
):
    _, tokens, width = queries.shape
    lanes = tokens * width // HD // HALVES
    local, length, _ = passage_keys.shape
    _, cite_count, picks = selected.shape
    chips = n // 2
    slots = local * PMOST
    bf, f32, i32 = jnp.bfloat16, jnp.float32, jnp.int32
    dma = pltpu.SemaphoreType.DMA
    tall = HD + ONES
    out_block = pltpu.VMEM((chips, HALVES, HD, lanes), bf)
    stat_block = pltpu.VMEM((chips, HALVES, 8, lanes), f32)
    kv_block = pltpu.VMEM((HALVES, kv, tokens // kv, width // HALVES), bf)
    return pl.pallas_call(
        functools.partial(fused_kernel, n, kv),
        out_shape=jax.ShapeDtypeStruct((1, tokens // kv, width * kv), bf),
        in_specs=[ANY] * 9,
        out_specs=VM,
        scratch_shapes=[
            pltpu.VMEM((8, 128), i32),
            pltpu.VMEM(citations.shape, i32),
            pltpu.VMEM(suffix_keys.shape, bf),
            pltpu.VMEM(suffix_values.shape, bf),
            pltpu.VMEM(fresh_keys.shape, bf),
            pltpu.VMEM(fresh_values.shape, bf),
            pltpu.VMEM(passage_keys.shape, bf),
            pltpu.VMEM(passage_values.shape, bf),
            pltpu.VMEM((local, tall, length), bf),
            pltpu.VMEM((n, tokens, width // HALVES), bf),
            pltpu.VMEM((n, tokens, width // HALVES), bf),
            pltpu.VMEM((n, 8, 128), i32),
            pltpu.VMEM((n, cite_count, picks), i32),
            pltpu.VMEM((slots, length, picks), bf),
            pltpu.VMEM((length, lanes), f32),
            pltpu.VMEM((length, lanes), f32),
            pltpu.VMEM((2, 8, lanes), f32),
            pltpu.VMEM((slots, tall, lanes), f32),
            pltpu.VMEM((slots, 8, lanes), f32),
            pltpu.VMEM((HALVES, tall, lanes), f32),
            pltpu.VMEM((HALVES, 8, lanes), f32),
            pltpu.VMEM((chips, HALVES, HD, lanes), f32),
            stat_block,
            *([out_block, stat_block] * 4),
            kv_block,
            kv_block,
            pltpu.SMEM((n, 8, 128), i32),
            pltpu.SMEM((slots,), i32),
            pltpu.SMEM((slots,), i32),
            pltpu.SMEM((n * local,), i32),
            pltpu.SMEM((n * local,), i32),
            dma((7,)),
            dma((4,)),
            *([dma((4, chips))] * 4),
            *([dma((2, HALVES, chips))] * 4),
            dma((HALVES, kv)),
            dma((HALVES, kv)),
        ],
        compiler_params=pltpu.CompilerParams(
            collective_id=0, has_side_effects=True, vmem_limit_bytes=LIMIT
        ),
        name="fused_attention",
    )(
        queries,
        suffix_keys,
        suffix_values,
        fresh_keys,
        fresh_values,
        passage_keys,
        passage_values,
        citations,
        selected,
    )


def solution(mesh):
    placed = (
        P("pass", None, "kv"),
        P("pass", None, "kv"),
        P("pass", None, "kv"),
        P("pass", None, "kv"),
        P("pass", None, "kv"),
        P("pass", None, None, "kv"),
        P("pass", None, None, "kv"),
        P("pass", None),
        P("pass", None, None),
    )
    return jax.shard_map(
        functools.partial(body, mesh.shape["pass"], mesh.shape["kv"]),
        mesh=mesh,
        in_specs=placed,
        out_specs=P("pass", "kv", None),
        check_vma=False,
    )
```
